32 devices in a mesh: gz: 4 (over z), gx: 4 (over y, core), gy: 2 (over x).
Axes of the slice: x: 2, y: 2, z: 4, core: 2. Of those that a mesh axis runs over, the one named last changes fastest.
Arguments:
- fields_in: float32 [6, 16, 256, 256], P(None, 'gz', 'gx', 'gy'), may hold values from -6 to 6
- material: int32 [16, 256, 256], P('gz', 'gx', 'gy'), may hold values from 0 to 3, as said below
- material_eps: float32 [4], replicated, may hold values from 1 to 12
- source_plane: int32 [1], replicated, may hold values from 0 to 15
- source_wave: float32 [4], replicated, may hold values from -8 to 8
- source_profile: float32 [256, 256], P('gx', 'gy'), may hold values from -6 to 6
- forward_fields: bfloat16 [4, 3, 16, 256, 256], P(None, None, 'gz', 'gx', 'gy'), may hold values from -6 to 6
Outputs:
- fields_out: float32 [6, 16, 256, 256], P(None, 'gz', 'gx', 'gy')
- eps_grad: float32 [16, 256, 256], P('gz', 'gx', 'gy')
The draws below stay inside these ranges and needn't reach their ends.
Inputs may be any that keep to these rules, and one draw needn't show every extreme that they name: `material`: planes z below 6 hold index 1; planes from 10 up hold index 0; the planes between hold 0 or an index of 2 to 3 in each cell.
All inputs are finite; a program needn't handle non-finite values.
Results may differ from the reference program's by a relative error of at most 0.0003.
Values sent between devices are 32-bit elements; how exact they have to be, the bound alone decides.
No kernel may reach another device: no remote copies, remote signals or barrier semaphores. Data moves between devices by JAX's collectives and lax.ppermute only.
A program may use at most 64 MiB of HBM per device.

```python
import jax
import jax.numpy as jnp

STEPS = 4
NMAT = 4
NX = 256
NY = 256
NZ = 16


def draw_material(key, part):
    zpos = jnp.arange(NZ)[:, None, None]
    lower = NZ // 2 - NZ // 8
    upper = NZ // 2 + NZ // 8
    picked = jax.random.randint(key, (NZ, NX, NY), 0, NMAT - 1)
    pillar = jnp.where(picked == 0, 0, picked + 1)
    layered = jnp.where(zpos < lower, 1, jnp.where(zpos < upper, pillar, 0))
    layered = layered.at[lower, 0, 0].set(NMAT - 1)
    return layered.astype(jnp.int32)


def levels(key, dims, pieces, least, top_value):
    def one(axis_at, parts):
        steps = jax.random.uniform(jax.random.fold_in(jax.random.fold_in(key, 6), axis_at), (parts,), jnp.float32, least / len(pieces), top_value / len(pieces))
        return jnp.repeat(jnp.exp(steps), dims[axis_at] // parts).reshape((-1,) + (1,) * (len(dims) - axis_at - 1))

    loudness = one(*pieces[0])
    for cut in pieces[1:]:
        loudness = loudness * one(*cut)
    return loudness


def normal_values(rng, shape, spread, limit, pieces=(), dtype=jnp.bfloat16):
    values = jax.random.normal(rng, shape, jnp.float32) * spread
    if len(pieces) > 0:
        values = levels(rng, shape, pieces, -0.22, 0.18) * values
    return jnp.clip(values, min=-limit, max=limit).astype(dtype)


def setup_inputs(seed: int = 0) -> dict:
    keys = jax.random.split(jax.random.key(seed), 8)
    return {
        "fields_in": normal_values(keys[0], (6, NZ, NX, NY), 1.0, 6.0, ((1, 4), (2, 4), (3, 2)), jnp.float32),
        "material": draw_material(jax.random.fold_in(keys[7], 71), 0),
        "material_eps": jnp.clip(jax.random.uniform(keys[2], (NMAT,), jnp.float32, 1.0, 12.0), 1.0, 12.0),
        "source_plane": jax.random.randint(keys[3], (1,), 0, NZ).astype(jnp.int32),
        "source_wave": normal_values(keys[4], (STEPS,), 2.0, 8.0, (), jnp.float32),
        "source_profile": normal_values(keys[5], (NX, NY), 1.0, 6.0, ((0, 4), (1, 2)), jnp.float32),
        "forward_fields": normal_values(keys[6], (STEPS, 3, NZ, NX, NY), 1.0, 6.0, ((2, 4), (3, 4), (4, 2))),
    }


COURANT = 0.5


def z_after(field):
    return jnp.concatenate([field[1:], jnp.zeros_like(field[:1])], axis=0)


def z_before(field):
    return jnp.concatenate([jnp.zeros_like(field[:1]), field[:-1]], axis=0)


def reference(fields_in, material, material_eps, source_plane, source_wave, source_profile, forward_fields):
    permit = material_eps[material]
    coef = COURANT / permit
    depth = material.shape[0]
    zpos = jnp.arange(depth).astype(jnp.int32)
    source = jnp.where(zpos == source_plane[0], 1.0, 0.0).astype(jnp.float32)[:, None, None] * source_profile[None]
    elec_x, elec_y, elec_z = fields_in[0], fields_in[1], fields_in[2]
    magn_x, magn_y, magn_z = fields_in[3], fields_in[4], fields_in[5]
    grad = jnp.zeros(material.shape, jnp.float32)
    for instant in range(source_wave.shape[0]):
        curl_x = (jnp.roll(elec_z, -1, 2) - elec_z) - (z_after(elec_y) - elec_y)
        curl_y = (z_after(elec_x) - elec_x) - (jnp.roll(elec_z, -1, 1) - elec_z)
        curl_z = (jnp.roll(elec_y, -1, 1) - elec_y) - (jnp.roll(elec_x, -1, 2) - elec_x)
        magn_x = magn_x - COURANT * curl_x
        magn_y = magn_y - COURANT * curl_y
        magn_z = magn_z - COURANT * curl_z
        back_x = (magn_z - jnp.roll(magn_z, 1, 2)) - (magn_y - z_before(magn_y))
        back_y = (magn_x - z_before(magn_x)) - (magn_z - jnp.roll(magn_z, 1, 1))
        back_z = (magn_y - jnp.roll(magn_y, 1, 1)) - (magn_x - jnp.roll(magn_x, 1, 2))
        elec_x = elec_x + coef * back_x + coef * source_wave[instant] * source
        elec_y = elec_y + coef * back_y
        elec_z = elec_z + coef * back_z
        stored = forward_fields[instant].astype(jnp.float32)
        grad = grad + stored[0] * elec_x + stored[1] * elec_y + stored[2] * elec_z
    fields_out = jnp.stack([elec_x, elec_y, elec_z, magn_x, magn_y, magn_z])
    eps_grad = jnp.where(material >= 2, -grad, 0.0).astype(jnp.float32)
    return fields_out, eps_grad
```

```python
import jax
import jax.numpy as jnp
from jax import lax
from jax.experimental import pallas as pl
from jax.experimental.pallas import tpu as pltpu
from jax.sharding import PartitionSpec as P

COURANT = 0.5
HALO = 4
BEYOND = 2
TILE = 8
GROUP = 16
WIDE = 32
TRACES = 2 * HALO
GROUPS = 1
F32 = jnp.float32


def lane_ids(shape):
    return lax.broadcasted_iota(jnp.int32, shape, 1)


def row_ids(shape):
    return lax.broadcasted_iota(jnp.int32, shape, 0)


def turn(value, shift, axis):
    shift = shift % value.shape[axis]
    if shift == 0:
        return value
    return pltpu.roll(value, shift, axis)


def x_after(value):
    return turn(value, -1, 0)


def x_before(value):
    return turn(value, 1, 0)


def swaps(size, periodic):
    first = [(i, i + 1) for i in range(0, size - 1, 2)]
    second = [(i, i + 1) for i in range(1, size - 1, 2)]
    if periodic and size > 2:
        second.append((size - 1, 0))
    both = lambda pairs: pairs + [(b, a) for a, b in pairs]
    return both(first), both(second)


def z_swaps(size, beside):
    first, second = swaps(size, False)
    wide = lambda pairs: [(a * beside + i, b * beside + i) for a, b in pairs for i in range(beside)]
    idle = [z for z in range(size) if all(z != a for a, _ in second)]
    cores = [(z * beside + i, z * beside + (i ^ 1)) for z in idle for i in range(beside)]
    return first, wide(first), second, wide(second) + cores


def pillars(depth, size):
    planes = depth * size
    return planes * 3 // 8, planes * 5 // 8


def sends_coef(depth, size, pairs):
    first, end = pillars(depth, size)
    edges = [max(a, b) * depth for a, b in pairs]
    return any(edge - BEYOND < end and edge + BEYOND > first for edge in edges)


def is_even(axis):
    return lax.rem(lax.axis_index(axis), 2) == 0


def coef_of(which, eps, count):
    permit = jnp.zeros(which.shape, F32)
    for index in range(count):
        permit = jnp.where(which == index, eps(index), permit)
    return (COURANT * COURANT) / permit


def slab_scale(c):
    return 1.0 / COURANT if 3 <= c < 6 else 1.0


def x_pack_kernel(
    fields, material, profile, eps, wave, to_a, to_b, scalars, fields_in, material_in, profile_in, eps_in, wave_in, sems
):
    depth, rows, lanes = material.shape
    pairs = ((fields, fields_in), (material, material_in), (profile, profile_in), (eps, eps_in), (wave, wave_in))
    copies = [pltpu.make_async_copy(one, two, sems.at[index]) for index, (one, two) in enumerate(pairs)]
    for copy in copies:
        copy.start()
    for copy in copies:
        copy.wait()
    even = is_even("gx")
    upper = row_ids((TILE, lanes)) < HALO

    def slab(side, s):
        c, z = divmod(s, depth)
        here = slice(0, TILE) if side == 0 else slice(rows - TILE, rows)
        if c < 6:
            return fields_in[c, z, here, :] * slab_scale(c)
        if c == 6:
            return coef_of(material_in[z, here, :], lambda index: eps_in[index], eps.shape[0])
        return profile_in[here, :]

    count = 7 * depth + 1
    for tile in range(to_a.shape[0]):
        one, two = 2 * tile, min(2 * tile + 1, count - 1)
        left = jnp.where(upper, slab(0, one), turn(slab(0, two), HALO, 0))
        right = jnp.where(upper, turn(slab(1, one), HALO, 0), slab(1, two))
        to_a[tile] = jnp.where(even, right, left)
        to_b[tile] = jnp.where(even, left, right)
    values = [wave_in[t] * (1.0 / COURANT) for t in range(HALO)] + [eps_in[i] for i in range(eps.shape[0])]
    for index, value in enumerate(values):
        scalars[index : index + 1, :] = jnp.full((1, lanes), value)


def y_pack_tile(slab, depth, lanes):
    quad = lane_ids((TILE, lanes)) // HALO
    low = jnp.zeros((TILE, lanes), F32)
    high = jnp.zeros((TILE, lanes), F32)
    for c in range(8):
        for z in range(depth):
            value = slab(c, z)
            at = WIDE * z + HALO * c
            low = jnp.where(quad == at // HALO, turn(value, at, 1), low)
            at = at + HALO
            high = jnp.where(quad == at // HALO % (lanes // HALO), turn(value, at + HALO, 1), high)
    return low, high


def y_place(out, at, low, high, both):
    here = pl.ds(at, TILE)
    if both:
        out[0, here, :], out[1, here, :] = low, high
    else:
        even = is_even("gy")
        out[0, here, :] = jnp.where(even, high, low)
        out[1, here, :] = jnp.where(even, low, high)


def x_unpack_kernel(from_a, from_b, partly, halo, out):
    depth = (halo.shape[0] - 1) // 7
    lanes = halo.shape[2]
    even = is_even("gx")
    upper = row_ids((TILE, lanes)) < HALO
    count = halo.shape[0]
    for tile in range(from_a.shape[0]):
        a, b = from_a[tile], from_b[tile]
        right = jnp.where(even, a, b)
        left = jnp.where(even, b, a)
        halo[2 * tile] = jnp.where(upper, right, turn(left, HALO, 0))
        if 2 * tile + 1 < count:
            halo[2 * tile + 1] = jnp.where(upper, turn(right, HALO, 0), left)
    slab = lambda c, z: halo[depth * c + z] if c < 7 else halo[7 * depth]
    low, high = y_pack_tile(slab, depth, lanes)
    y_place(out, out.shape[1] - TILE, low, high, lax.axis_size("gy") == 2)


def plane_amount(table, instant, z, depth):
    at = instant * (depth + 2) + z
    return table[at : at + 1, :]


def curl_of_electric(ex, ey, ez, y_ex, y_ez, z_ex, z_ey):
    curl_x = (y_ez - ez) - (z_ey - ey)
    curl_y = (z_ex - ex) - (x_after(ez) - ez)
    curl_z = (x_after(ey) - ey) - (y_ex - ex)
    return curl_x, curl_y, curl_z


def curl_of_magnetic(hx, hy, hz, y_hx, y_hz, z_hx, z_hy):
    back_x = (hz - y_hz) - (hy - z_hy)
    back_y = (hx - z_hx) - (hz - x_before(hz))
    back_z = (hy - x_before(hy)) - (hx - y_hx)
    return back_x, back_y, back_z


def alone_planes(depth, instant):
    every = list(range(depth))
    left = HALO - 1 - instant
    if left == 0:
        return [depth - 1], []
    if left == 1:
        return sorted({0, depth - 2, depth - 1} & set(every)), sorted({0, depth - 1})
    return every, every


def alone_magnetic(main, instant, depth):
    planes = alone_planes(depth, instant)[0]
    shifted = {p: (turn(main[0, p], -1, 1), turn(main[2, p], -1, 1)) for p in planes}
    for p in planes:
        ex, ey, ez = main[0, p], main[1, p], main[2, p]
        zero = jnp.zeros_like(ex)
        z_ex, z_ey = (main[0, p + 1], main[1, p + 1]) if p + 1 < depth else (zero, zero)
        curl = curl_of_electric(ex, ey, ez, *shifted[p], z_ex, z_ey)
        for c in range(2 if instant == HALO - 1 else 3):
            main[3 + c, p] = main[3 + c, p] - curl[c]


def alone_electric(main, instant, depth, coef, source):
    planes = alone_planes(depth, instant)[1]
    shifted = {p: (turn(main[3, p], 1, 1), turn(main[5, p], 1, 1)) for p in planes}
    for p in planes:
        hx, hy, hz = main[3, p], main[4, p], main[5, p]
        zero = jnp.zeros_like(hx)
        z_hx, z_hy = (main[3, p - 1], main[4, p - 1]) if p > 0 else (zero, zero)
        back = curl_of_magnetic(hx, hy, hz, *shifted[p], z_hx, z_hy)
        here = coef(p)
        main[0, p] = main[0, p] + here * (back[0] + source(p))
        main[1, p] = main[1, p] + here * back[1]
        main[2, p] = main[2, p] + here * back[2]


def interior_kernel(
    fields, material, profile, scalars, plane, coef, to_a, to_b, y_out, table, main
):
    depth, rows, lanes = material.shape
    eps = lambda index: scalars[HALO + index : HALO + index + 1, :]
    lane = lane_ids((1, lanes))
    there = plane[...] - lax.axis_index("gz") * depth
    inside = jnp.logical_and(there >= 0, there < depth)
    groups = [jnp.full((1, lanes), z, jnp.int32) for z in range(depth)]
    groups += [lane // WIDE, lane // GROUP - BEYOND]
    for instant in range(HALO):
        amount = jnp.where(inside, scalars[instant : instant + 1, :], 0.0)
        for index, group in enumerate(groups):
            at = instant * len(groups) + index
            table[at : at + 1, :] = jnp.where(group == there, amount, 0.0)
    base = HALO * len(groups)
    count = scalars.shape[0] - HALO
    table[base : base + count, :] = scalars[HALO : HALO + count, :]
    for z in range(depth):
        coef[z] = coef_of(material[z], eps, count)
        for c in range(6):
            value = fields[c, z]
            main[c, z] = value * slab_scale(c) if c >= 3 else value

    even = is_even("gz")

    def send(item, upward, downward):
        if item < to_a.shape[0]:
            to_a[item] = jnp.where(even, upward, downward)
        if item < to_b.shape[0]:
            to_b[item] = jnp.where(even, downward, upward)

    for beyond in range(BEYOND):
        send(TRACES + beyond, coef[depth - 1 - beyond], coef[beyond])
    for at in range(0, rows, TILE):
        here = pl.ds(at, TILE)

        def slab(c, z):
            if c < 6:
                return main[c, z, here, :]
            return coef[z, here, :] if c == 6 else profile[here, :]

        low, high = y_pack_tile(slab, depth, lanes)
        y_place(y_out, at, low, high, lax.axis_size("gy") == 2)
    for instant in range(HALO):
        alone_magnetic(main, instant, depth)
        for c in range(2):
            send(2 * instant + c, main[3 + c, depth - 1], main[c, 0])
        if instant < HALO - 1:
            alone_electric(
                main,
                instant,
                depth,
                lambda p: coef[p],
                lambda p: plane_amount(table, instant, p, depth) * profile[...],
            )


def own_strips_kernel(fields, coef, profile, halo, strips):
    depth, rows, lanes = coef.shape
    for at in range(0, rows + TILE, TILE):
        here = pl.ds(at, TILE)
        lane = lane_ids((TILE, lanes))
        part = lax.rem(lane, WIDE) // HALO
        on_right = jnp.logical_or(part == 1, part == 2)
        for c in range(8):
            out = jnp.zeros((TILE, lanes), F32)
            for z in range(depth):
                if at == rows:
                    value = halo[depth * c + z] if c < 7 else halo[7 * depth]
                elif c < 6:
                    value = fields[c, z, here, :] * slab_scale(c)
                else:
                    value = coef[z, here, :] if c == 6 else profile[here, :]
                first = WIDE * z + HALO
                both = jnp.where(on_right, turn(value, first + 2 * HALO, 1), turn(value, first + 4 * HALO, 1))
                out = jnp.where(lane // WIDE == z, both, out)
            strips[c, here, :] = out


def frame_kernel(
    fields, coef, profile, table, halo, own, from_one, from_two, strips, to_a, to_b, main, cells, strip
):
    depth, rows, lanes = coef.shape
    wide = rows + TILE
    shape = (wide, lanes)
    lane = lane_ids(shape)
    quad = lane // HALO
    part = lax.rem(quad, WIDE // HALO)
    if lax.axis_size("gy") == 2:
        from_right, from_left = from_one[...], from_two[...]
    else:
        even = is_even("gy")
        from_right = jnp.where(even, from_one[...], from_two[...])
        from_left = jnp.where(even, from_two[...], from_one[...])
    is_halo = jnp.logical_or(part == 3, part == 4)
    mixed = (
        jnp.where(lax.rem(quad, 2) == 0, from_right, from_left),
        jnp.where(lax.rem(quad, 2) == 0, from_left, from_right),
    )
    for c in range(8):
        value = jnp.where(is_halo, turn(mixed[c % 2], 3 * HALO - HALO * c, 1), own[c])
        strips[c] = value
        if c < 6:
            strip[c] = value
    ends = (slice(0, TILE), slice(TILE, 2 * TILE), slice(2 * TILE, 3 * TILE))
    last, first = pl.ds(rows - TILE, TILE), pl.ds(0, TILE)
    for z in range(depth):
        for c in range(6):
            main[c, z, ends[0], :] = fields[c, z, last, :] * slab_scale(c)
            main[c, z, ends[1], :] = halo[depth * c + z]
            main[c, z, ends[2], :] = fields[c, z, first, :] * slab_scale(c)
        cells[z, ends[0], :] = coef[z, last, :]
        cells[z, ends[1], :] = halo[6 * depth + z]
        cells[z, ends[2], :] = coef[z, first, :]
    cells[depth, ends[0], :] = profile[last, :]
    cells[depth, ends[1], :] = halo[7 * depth]
    cells[depth, ends[2], :] = profile[first, :]

    even = is_even("gz")
    bottom, top = lane < WIDE, lane >= WIDE * (depth - 1)
    upward = jnp.zeros(shape, F32)
    downward = jnp.zeros(shape, F32)

    for instant in range(HALO):
        alone_magnetic(main, instant, depth)
        ex, ey, ez = strip[0], strip[1], strip[2]
        z_ex = jnp.where(top, 0.0, turn(ex, -WIDE, 1))
        z_ey = jnp.where(top, 0.0, turn(ey, -WIDE, 1))
        curl = curl_of_electric(ex, ey, ez, turn(ex, -1, 1), turn(ez, -1, 1), z_ex, z_ey)
        for c in range(2 if instant == HALO - 1 else 3):
            strip[3 + c] = strip[3 + c] - curl[c]
        for c in range(2):
            item = 2 * instant + c
            here = lane // GROUP == item
            upward = jnp.where(here, turn(strip[3 + c], GROUP * item - WIDE * (depth - 1) - TILE, 1), upward)
            downward = jnp.where(here, turn(strip[c], GROUP * item - TILE, 1), downward)
            rows_at = wide + TILE * item
            ups = main[3 + c, depth - 1]
            downs = main[c, 0]
            for part_at, up_at, down_at in (
                (rows_at, TILE - instant - 1, TILE - instant),
                (rows_at + HALO, TILE + HALO + instant + 1, TILE + HALO + instant),
            ):
                up = ups[up_at : up_at + HALO, :]
                down = downs[down_at : down_at + HALO, :]
                to_a[part_at : part_at + HALO, :] = jnp.where(even, up, down)
                to_b[part_at : part_at + HALO, :] = jnp.where(even, down, up)
        if instant == HALO - 1:
            break
        alone_electric(
            main,
            instant,
            depth,
            lambda p: cells[p],
            lambda p: plane_amount(table, instant, p, depth) * cells[depth],
        )
        hx, hy, hz = strip[3], strip[4], strip[5]
        z_hx = jnp.where(bottom, 0.0, turn(hx, WIDE, 1))
        z_hy = jnp.where(bottom, 0.0, turn(hy, WIDE, 1))
        back = curl_of_magnetic(hx, hy, hz, turn(hx, 1, 1), turn(hz, 1, 1), z_hx, z_hy)
        amount = plane_amount(table, instant, depth, depth)
        strip[0] = strip[0] + strips[6] * (back[0] + amount * strips[7])
        strip[1] = strip[1] + strips[6] * back[1]
        strip[2] = strip[2] + strips[6] * back[2]
    to_a[0:wide, :] = jnp.where(even, upward, downward)
    to_b[0:wide, :] = jnp.where(even, downward, upward)
    def send(at, up, down):
        if at < to_a.shape[0]:
            to_a[at : at + TILE, :] = jnp.where(even, up, down)
        if at < to_b.shape[0]:
            to_b[at : at + TILE, :] = jnp.where(even, down, up)

    at = wide + TILE * TRACES
    for beyond in range(BEYOND):
        send(at, halo[6 * depth + depth - 1 - beyond], halo[6 * depth + beyond])
        at += TILE
    side = lanes // (BEYOND * GROUP)
    tile_lane = lane_ids((TILE, lanes))
    for begin in range(0, wide // TILE, side):
        up = jnp.zeros((TILE, lanes), F32)
        down = jnp.zeros((TILE, lanes), F32)
        for tile in range(begin, min(begin + side, wide // TILE)):
            value = strips[6, TILE * tile : TILE * (tile + 1), :]
            for beyond in range(BEYOND):
                goal = GROUP * (BEYOND * (tile - begin) + beyond)
                here = tile_lane // GROUP == goal // GROUP
                z = depth - BEYOND + beyond
                up = jnp.where(here, turn(value, goal - WIDE * z - TILE, 1), up)
                down = jnp.where(here, turn(value, goal - WIDE * beyond - TILE, 1), down)
        send(at, up, down)
        at += TILE


def received(a, b, above, here):
    even = is_even("gz")
    one, two = (a, b) if above else (b, a)
    place = lax.axis_index("gz")
    exists = place < lax.axis_size("gz") - 1 if above else place > 0
    return jnp.where(exists, jnp.where(even, one[here], two[here]), 0.0)


def coef_beyond(a, b, above, p, depth, table, shape):
    size = lax.axis_size("gz")
    first, end = pillars(depth, size)
    z = lax.axis_index("gz") * depth + p - BEYOND
    base = HALO * (depth + 2)
    quarter = COURANT * COURANT
    low, high = quarter / table[base + 1 : base + 2, :], quarter / table[base : base + 1, :]
    layer = jnp.broadcast_to(jnp.where(z < first, low, high), shape)
    one = layer if a is None else a()
    two = layer if b is None else b()
    even = is_even("gz")
    value = jnp.where(even, one, two) if above else jnp.where(even, two, one)
    return jnp.where(jnp.logical_and(z >= 0, z < depth * size), value, 0.0)


def edges_after(ex_shifted, ez, lane):
    return jnp.where(lax.rem(lane, GROUP) == HALO - 1, ex_shifted, ez)


def edges_before(hx_shifted, hz, lane):
    return jnp.where(lax.rem(lane, GROUP) == 3 * HALO, hx_shifted, hz)


def arrived_kernel(*refs):
    pass


def prepare_kernel(wide_strips, early, strips, out):
    _, wide, lanes = wide_strips.shape
    depth = lanes // WIDE
    lane = lane_ids((TILE, lanes))
    for at in range(0, wide, TILE):
        here = pl.ds(at, TILE)
        for c in range(8):
            value = wide_strips[c, here, :]
            moved = jnp.zeros((TILE, lanes), F32)
            for z in range(depth):
                goal = GROUP * (z + BEYOND)
                moved = jnp.where(lane // GROUP == z + BEYOND, turn(value, goal - WIDE * z - TILE, 1), moved)
            strips[c, here, :] = moved


def window_kernel(
    fields,
    coef,
    profile,
    halo,
    table,
    strips,
    early_a,
    early_b,
    late_a,
    late_b,
    forward,
    material,
    fields_out,
    eps_grad,
    results,
    grad,
    beside,
    sems,
):
    depth, rows, lanes = material.shape
    wide = rows + TILE
    shape = (wide, lanes)
    own = range(BEYOND, BEYOND + depth)
    first, last = own[0], own[-1]
    lane = lane_ids(shape)
    group = lane // GROUP

    late_strips = [received(late_a, late_b, above, slice(0, wide)) for above in (False, True)]
    for side, above in enumerate((False, True)):
        for item in range(TRACES):
            lost = item // 2 if above else item // 2 + 1
            beside[side, item, 0:rows, :] = received(early_a, early_b, above, item)
            at = wide + TILE * item
            right = received(late_a, late_b, above, slice(at, at + HALO))
            left = received(late_a, late_b, above, slice(at + HALO, at + TILE))
            beside[side, item, rows - lost : rows - lost + HALO, :] = right
            if lost < HALO:
                beside[side, item, rows + HALO + lost : wide, :] = left[0 : HALO - lost]
            if lost > 0:
                beside[side, item, 0:lost, :] = left[HALO - lost : HALO]
                value = beside[side, item]
                edge = turn(late_strips[side], lanes - HALO - GROUP * item, 1)
                value = jnp.where(lane >= lanes - lost, edge, value)
                lost_left = lost if above else lost - 1
                if lost_left > 0:
                    edge = turn(late_strips[side], -(GROUP * item + 3 * HALO), 1)
                    value = jnp.where(lane < lost_left, edge, value)
                beside[side, item] = value

    def trace(above, item):
        return beside[1 if above else 0, item]

    def strip_trace(above, item):
        p = last + 1 if above else first - 1
        return jnp.where(group == p, turn(late_strips[above], GROUP * (p - item), 1), 0.0)

    at = wide + TILE * TRACES
    lates = [late if late.shape[0] > at else None for late in (late_a, late_b)]
    joined = lambda top, tile: jnp.concatenate([top, tile], axis=0)
    zero = jnp.zeros(shape, F32)

    def late_tile(here, shift=0):
        return [None if late is None else (lambda late=late: turn(late[here], shift, 1)) for late in lates]

    wide_coef = {first + z: joined(coef[z], halo[6 * depth + z]) for z in range(depth)}
    for beyond in range(BEYOND):
        for above in (False, True):
            p = last + 1 + beyond if above else first - 1 - beyond
            item = TRACES + beyond
            parts = [
                None if early.shape[0] == TRACES else (lambda early=early: early[item])
                for early in (early_a, early_b)
            ]
            top = coef_beyond(*parts, above, p, depth, table, (rows, lanes))
            parts = late_tile(slice(at, at + TILE))
            wide_coef[p] = joined(top, coef_beyond(*parts, above, p, depth, table, (TILE, lanes)))
        at += TILE
    side = lanes // (BEYOND * GROUP)
    tile_group = lane_ids((TILE, lanes)) // GROUP
    tiles = []
    for tile in range(wide // TILE):
        here = slice(at + TILE * (tile // side), at + TILE * (tile // side) + TILE)
        start = BEYOND * GROUP * (tile % side)
        value = strips[6, TILE * tile : TILE * (tile + 1), :]
        low = coef_beyond(*late_tile(here, -start), False, tile_group, depth, table, (TILE, lanes))
        parts = late_tile(here, GROUP * (last + 1) - start)
        high = coef_beyond(*parts, True, tile_group, depth, table, (TILE, lanes))
        value = jnp.where(tile_group < first, low, value)
        tiles.append(jnp.where(tile_group > last, high, value))
    strip_coef = jnp.concatenate(tiles, axis=0)
    wide_profile = joined(profile[...], halo[7 * depth])
    strip = [strips[c] for c in range(6)]
    main = {}
    for c in range(6):
        for p in range(first - BEYOND, last + BEYOND + 1):
            z = p - first
            main[c, p] = joined(fields[c, z], halo[depth * c + z]) if first <= p <= last else zero
            if 3 <= c and first <= p <= last:
                main[c, p] = joined(fields[c, z] * slab_scale(c), halo[depth * c + z])
    below_factor = jnp.where(lax.axis_index("gz") > 0, 1.0, 0.0)
    strip_factor = jnp.where(group < first, below_factor, 1.0)

    copies = []

    def hand_out(source, target):
        copy = pltpu.make_async_copy(source, target, sems.at[len(copies)])
        copy.start()
        copies.append(copy)

    def magnetic_planes(instant):
        above = min(instant, HALO - 1 - instant, BEYOND - 1)
        return list(range(first - min(instant + 1, HALO - instant, BEYOND), last + above + 1))

    def electric_planes(instant):
        reach = min(instant + 1, HALO - 1 - instant, BEYOND)
        return list(range(first - reach, last + reach + 1))

    def in_groups(planes):
        size = -(-len(planes) // GROUPS)
        return [planes[at : at + size] for at in range(0, len(planes), size)]

    def rolled_after(mixed, planes):
        edge = {p: turn(mixed, -(GROUP * p + HALO), 1) for p in planes}
        ex = {p: turn(main[0, p], -1, 1) for p in planes}
        ez = {p: turn(jnp.where(lane == 0, edge[p], main[2, p]), -1, 1) for p in planes}
        return {p: (jnp.where(lane == lanes - 1, edge[p], ex[p]), ez[p]) for p in planes}

    def rolled_before(mixed, planes):
        edge = {p: turn(mixed, -(GROUP * p + 3 * HALO), 1) for p in planes}
        hx = {p: turn(main[3, p], 1, 1) for p in planes}
        hz = {p: turn(jnp.where(lane == lanes - 1, edge[p], main[5, p]), 1, 1) for p in planes}
        return {p: (jnp.where(lane == 0, edge[p], hx[p]), hz[p]) for p in planes}

    def strip_magnetic(instant):
        ex, ey, ez = strip[0:3]
        curl = curl_of_electric(ex, ey, ez, *strip_shifts)
        for c in range(3):
            strip[3 + c] = strip[3 + c] - strip_factor * curl[c]
        hx, hy, hz = strip[3:6]
        y_hx, y_hz = turn(hx, 1, 1), turn(hz, 1, 1)
        z_hx = turn(hx + strip_trace(False, 2 * instant), GROUP, 1)
        z_hy = turn(hy + strip_trace(False, 2 * instant + 1), GROUP, 1)
        return (y_hx, y_hz, z_hx, z_hy), edges_before(y_hx, hz, lane)

    def strip_shifted_electric(instant):
        ex, ey, ez = strip[0:3]
        y_ex, y_ez = turn(ex, -1, 1), turn(ez, -1, 1)
        z_ex = turn(ex + strip_trace(True, 2 * instant), -GROUP, 1)
        z_ey = turn(ey + strip_trace(True, 2 * instant + 1), -GROUP, 1)
        return (y_ex, y_ez, z_ex, z_ey), edges_after(y_ex, ez, lane)

    def strip_electric(instant):
        back = curl_of_magnetic(*strip[3:6], *strip_shifts)
        amount = plane_amount(table, instant, depth + 1, depth)
        strip[0] = strip[0] + strip_coef * (back[0] + amount * strips[7])
        strip[1] = strip[1] + strip_coef * back[1]
        strip[2] = strip[2] + strip_coef * back[2]
        return strip_shifted_electric(instant + 1)

    total = [None] * depth
    strip_shifts, mixed = strip_shifted_electric(0)
    moved = rolled_after(mixed, list(own))
    strip_shifts, mixed = strip_magnetic(0)
    for instant in range(HALO):
        item = 2 * instant
        final = instant == HALO - 1

        mixed_now = mixed
        if not final:
            strip_shifts, mixed = strip_electric(instant)
        following = electric_planes(instant)
        later = {p: (zero, zero) for p in following}
        for planes in in_groups(magnetic_planes(instant)):
            for p in planes:
                z_ex, z_ey = main[0, p + 1], main[1, p + 1]
                if p == last:
                    z_ex, z_ey = z_ex + trace(True, item), z_ey + trace(True, item + 1)
                curl = curl_of_electric(
                    main[0, p], main[1, p], main[2, p], *moved.get(p, (zero, zero)), z_ex, z_ey
                )
                for c in range(3):
                    main[3 + c, p] = main[3 + c, p] - (curl[c] if p >= first else below_factor * curl[c])
                    if final and first <= p <= last:
                        results[3 + c, p - first] = main[3 + c, p][0:rows] * COURANT
                if final and first <= p <= last:
                    z = p - first
                    hand_out(results.at[pl.ds(3, 3), z], fields_out.at[pl.ds(3, 3), z])
            later.update(rolled_before(mixed_now, [p for p in planes if p in following]))
        moved = later

        mixed_now = mixed
        if not final:
            strip_shifts, mixed = strip_magnetic(instant + 1)
        following = [] if final else magnetic_planes(instant + 1)
        later = {}
        for planes in in_groups(electric_planes(instant)):
            for p in planes:
                z_hx, z_hy = main.get((3, p - 1), zero), main.get((4, p - 1), zero)
                if p == first:
                    z_hx, z_hy = z_hx + trace(False, item), z_hy + trace(False, item + 1)
                back = curl_of_magnetic(main[3, p], main[4, p], main[5, p], *moved[p], z_hx, z_hy)
                here = wide_coef[p]
                inside = first <= p <= last
                z = p - first
                if inside:
                    push = plane_amount(table, instant, z, depth) * wide_profile
                    back = (back[0] + push, back[1], back[2])
                for c in range(3):
                    main[c, p] = main[c, p] + here * back[c]
                    if inside:
                        term = forward[instant, c, z].astype(F32) * main[c, p][0:rows]
                        total[z] = term if total[z] is None else total[z] + term
                if inside and final:
                    for c in range(3):
                        results[c, z] = main[c, p][0:rows]
                    grad[z] = jnp.where(material[z] >= 2, -total[z], 0.0)
                    hand_out(results.at[pl.ds(0, 3), z], fields_out.at[pl.ds(0, 3), z])
                    hand_out(grad.at[z], eps_grad.at[z])
            later.update(rolled_after(mixed_now, [p for p in planes if p in following]))
        moved = later
    for copy in copies:
        copy.wait()


VMEM = pl.BlockSpec(memory_space=pltpu.VMEM)
FAR = pl.BlockSpec(memory_space=pltpu.HBM)


def near(array):
    return pltpu.with_memory_space_constraint(array, pltpu.VMEM)


def far_off(array):
    return pltpu.with_memory_space_constraint(array, pltpu.HBM), FAR


def call(kernel, operands, outs, scratch=(), far=0, aliases=None, name=None, cost=None):
    specs, arrays = [], []
    for operand in operands:
        if isinstance(operand, tuple):
            specs.append(operand[1])
            arrays.append(operand[0])
        else:
            specs.append(VMEM)
            arrays.append(near(operand))
    return pl.pallas_call(
        kernel,
        out_shape=[jax.ShapeDtypeStruct(s, F32) for s in outs[:far]] + [
            pltpu.VMEM(getattr(s, "shape", s), getattr(s, "dtype", F32)) for s in outs[far:]
        ],
        in_specs=specs,
        out_specs=[FAR] * far + [VMEM] * (len(outs) - far),
        scratch_shapes=[s if not isinstance(s, tuple) else pltpu.VMEM(s, F32) for s in scratch],
        input_output_aliases=aliases or {},
        compiler_params=pltpu.CompilerParams(vmem_limit_bytes=32 * 1024 * 1024),
        cost_estimate=cost,
        name=name,
    )(*arrays)


def on_device(
    fields_in, material, material_eps, source_plane, source_wave, source_profile, forward_fields
):
    depth, rows, lanes = material.shape
    assert source_wave.shape[0] == HALO and depth * WIDE == lanes and BEYOND <= depth
    assert (depth + 2 * BEYOND) * GROUP == lanes and TRACES * GROUP == lanes
    wide = rows + TILE
    slabs = 7 * depth + 1
    tiles = (slabs + 1) // 2

    inputs = (fields_in, material, source_profile, material_eps, source_wave)
    to_a, to_b, scalars, fields_in, material, source_profile = call(
        x_pack_kernel,
        [far_off(array) for array in inputs],
        [(tiles, TILE, lanes)] * 2
        + [(HALO + material_eps.shape[0], lanes), fields_in.shape, material, source_profile.shape],
        [
            pltpu.SMEM(material_eps.shape, F32),
            pltpu.SMEM(source_wave.shape, F32),
            pltpu.SemaphoreType.DMA((5,)),
        ],
        name="x_pack",
    )
    swap_a, swap_b = swaps(lax.axis_size("gx"), True)
    from_a = lax.ppermute(to_a, "gx", swap_a)
    from_b = lax.ppermute(to_b, "gx", swap_b)

    pairs_a, z_a, pairs_b, z_b = z_swaps(lax.axis_size("gz"), lax.axis_size("gx"))
    with_coef = [sends_coef(depth, lax.axis_size("gz"), pairs) for pairs in (pairs_a, pairs_b)]
    items = [TRACES + BEYOND * sent for sent in with_coef]
    plane = jnp.broadcast_to(source_plane[None], (1, lanes))
    coef, early_a, early_b, partly, table = call(
        interior_kernel,
        [fields_in, material, source_profile, scalars, plane],
        [(depth, rows, lanes)]
        + [(count, rows, lanes) for count in items]
        + [(2, wide, lanes), (HALO * (depth + 2) + material_eps.shape[0], lanes)],
        [(6, depth, rows, lanes)],
        name="interior",
    )
    halo, y_out = call(
        x_unpack_kernel,
        [from_a, from_b, partly],
        [(slabs, TILE, lanes), (2, wide, lanes)],
        aliases={2: 1},
        name="x_unpack",
    )
    swap_a, swap_b = swaps(lax.axis_size("gy"), True)
    if lax.axis_size("gy") == 2:
        both = lax.ppermute(y_out, "gy", swap_a)
        from_one, from_two = both[0], both[1]
    else:
        from_one = lax.ppermute(y_out[0], "gy", swap_a)
        from_two = lax.ppermute(y_out[1], "gy", swap_b)

    early_a = lax.ppermute(early_a, ("gz", "gx"), z_a)
    early_b = lax.ppermute(early_b, ("gz", "gx"), z_b)
    (own,) = call(
        own_strips_kernel,
        [fields_in, coef, source_profile, halo],
        [(8, wide, lanes)],
        name="own_strips",
    )
    side = lanes // (BEYOND * GROUP)
    coef_rows = TILE * BEYOND + TILE * (-(-wide // TILE // side))
    late_rows = [wide + TILE * TRACES + coef_rows * sent for sent in with_coef]
    strips, late_a, late_b = call(
        frame_kernel,
        [fields_in, coef, source_profile, table, halo, own, from_one, from_two],
        [(8, wide, lanes)] + [(count, lanes) for count in late_rows],
        [(6, depth, 3 * TILE, lanes), (depth + 1, 3 * TILE, lanes), (6, wide, lanes)],
        name="frame",
    )
    late_a = lax.ppermute(late_a, ("gz", "gx"), z_a)
    late_b = lax.ppermute(late_b, ("gz", "gx"), z_b)

    (early_b,) = call(
        arrived_kernel,
        [early_b],
        [early_b.shape],
        aliases={0: 0},
        name="arrived",
        cost=pl.CostEstimate(flops=10**9, bytes_accessed=0, transcendentals=0),
    )
    strips, early_b = call(
        prepare_kernel,
        [strips, early_b],
        [(8, wide, lanes), early_b.shape],
        aliases={1: 1},
        name="prepare",
    )
    fields_out, eps_grad = call(
        window_kernel,
        [fields_in, coef, source_profile, halo, table, strips, early_a, early_b, late_a, late_b]
        + [forward_fields, material],
        [(6, depth, rows, lanes), (depth, rows, lanes)],
        [
            (6, depth, rows, lanes),
            (depth, rows, lanes),
            (2, TRACES, wide, lanes),
            pltpu.SemaphoreType.DMA((3 * depth,)),
        ],
        far=2,
        name="window",
    )
    return (fields_out, eps_grad)


def solution(mesh):
    placed = (
        P(None, "gz", "gx", "gy"),
        P("gz", "gx", "gy"),
        P(),
        P(),
        P(),
        P("gx", "gy"),
        P(None, None, "gz", "gx", "gy"),
    )
    return jax.shard_map(
        on_device,
        mesh=mesh,
        in_specs=placed,
        out_specs=(P(None, "gz", "gx", "gy"), P("gz", "gx", "gy")),
        check_vma=False,
    )
```

```python
import jax
import jax.numpy as jnp
from jax import lax
from jax.experimental import pallas as pl
from jax.experimental.pallas import tpu as pltpu
from jax.sharding import PartitionSpec as P

COURANT = 0.5
HALO = 4
BEYOND = 2
TILE = 8
GROUP = 16
WIDE = 32
TRACES = 2 * HALO
GROUPS = 1
F32 = jnp.float32


def lane_ids(shape):
    return lax.broadcasted_iota(jnp.int32, shape, 1)


def row_ids(shape):
    return lax.broadcasted_iota(jnp.int32, shape, 0)


def turn(value, shift, axis):
    shift = shift % value.shape[axis]
    if shift == 0:
        return value
    return pltpu.roll(value, shift, axis)


def x_after(value):
    return turn(value, -1, 0)


def x_before(value):
    return turn(value, 1, 0)


def early_rows(rows):
    places, at = [], 0
    for item in range(TRACES):
        cut = item // 2
        places.append((at, cut, rows - cut))
        at += rows - 2 * cut
    return places, at


def swaps(size, periodic):
    first = [(i, i + 1) for i in range(0, size - 1, 2)]
    second = [(i, i + 1) for i in range(1, size - 1, 2)]
    if periodic and size > 2:
        second.append((size - 1, 0))
    both = lambda pairs: pairs + [(b, a) for a, b in pairs]
    return both(first), both(second)


def z_swaps(size, beside):
    first, second = swaps(size, False)
    wide = lambda pairs: [(a * beside + i, b * beside + i) for a, b in pairs for i in range(beside)]
    idle = [z for z in range(size) if all(z != a for a, _ in second)]
    cores = [(z * beside + i, z * beside + (i ^ 1)) for z in idle for i in range(beside)]
    return first, wide(first), second, wide(second) + cores


def pillars(depth, size):
    planes = depth * size
    return planes * 3 // 8, planes * 5 // 8


def sends_coef(depth, size, pairs):
    first, end = pillars(depth, size)
    edges = [max(a, b) * depth for a, b in pairs]
    return any(edge - BEYOND < end and edge + BEYOND > first for edge in edges)


def is_even(axis):
    return lax.rem(lax.axis_index(axis), 2) == 0


def coef_of(which, eps, count):
    permit = jnp.zeros(which.shape, F32)
    for index in range(count):
        permit = jnp.where(which == index, eps(index), permit)
    return (COURANT * COURANT) / permit


def slab_scale(c):
    return 1.0 / COURANT if 3 <= c < 6 else 1.0


def x_pack_kernel(
    fields, material, profile, eps, wave, to_a, to_b, scalars, fields_in, material_in, profile_in, eps_in, wave_in, sems
):
    depth, rows, lanes = material.shape
    pairs = ((fields, fields_in), (material, material_in), (profile, profile_in), (eps, eps_in), (wave, wave_in))
    copies = [pltpu.make_async_copy(one, two, sems.at[index]) for index, (one, two) in enumerate(pairs)]
    for copy in copies:
        copy.start()
    for copy in copies:
        copy.wait()
    even = is_even("gx")
    upper = row_ids((TILE, lanes)) < HALO

    def slab(side, s):
        c, z = divmod(s, depth)
        here = slice(0, TILE) if side == 0 else slice(rows - TILE, rows)
        if c < 6:
            return fields_in[c, z, here, :] * slab_scale(c)
        if c == 6:
            return coef_of(material_in[z, here, :], lambda index: eps_in[index], eps.shape[0])
        return profile_in[here, :]

    count = 7 * depth + 1
    for tile in range(to_a.shape[0]):
        one, two = 2 * tile, min(2 * tile + 1, count - 1)
        left = jnp.where(upper, slab(0, one), turn(slab(0, two), HALO, 0))
        right = jnp.where(upper, turn(slab(1, one), HALO, 0), slab(1, two))
        to_a[tile] = jnp.where(even, right, left)
        to_b[tile] = jnp.where(even, left, right)
    values = [wave_in[t] * (1.0 / COURANT) for t in range(HALO)] + [eps_in[i] for i in range(eps.shape[0])]
    for index, value in enumerate(values):
        scalars[index : index + 1, :] = jnp.full((1, lanes), value)


def y_pack_tile(slab, depth, lanes):
    quad = lane_ids((TILE, lanes)) // HALO
    low = jnp.zeros((TILE, lanes), F32)
    high = jnp.zeros((TILE, lanes), F32)
    for c in range(8):
        for z in range(depth):
            value = slab(c, z)
            at = WIDE * z + HALO * c
            moved = turn(value, at, 1)
            low = jnp.where(quad == at // HALO, moved, low)
            high = jnp.where(quad == (at // HALO - 1) % (lanes // HALO), moved, high)
    return low, high


def y_place(out, at, low, high, both):
    here = pl.ds(at, TILE)
    if both:
        out[0, here, :], out[1, here, :] = low, high
    else:
        even = is_even("gy")
        out[0, here, :] = jnp.where(even, high, low)
        out[1, here, :] = jnp.where(even, low, high)


def x_unpack_kernel(from_a, from_b, partly, halo, out):
    depth = (halo.shape[0] - 1) // 7
    lanes = halo.shape[2]
    even = is_even("gx")
    upper = row_ids((TILE, lanes)) < HALO
    count = halo.shape[0]
    for tile in range(from_a.shape[0]):
        a, b = from_a[tile], from_b[tile]
        right = jnp.where(even, a, b)
        left = jnp.where(even, b, a)
        halo[2 * tile] = jnp.where(upper, right, turn(left, HALO, 0))
        if 2 * tile + 1 < count:
            halo[2 * tile + 1] = jnp.where(upper, turn(right, HALO, 0), left)
    slab = lambda c, z: halo[depth * c + z] if c < 7 else halo[7 * depth]
    low, high = y_pack_tile(slab, depth, lanes)
    y_place(out, out.shape[1] - TILE, low, high, lax.axis_size("gy") == 2)


def plane_amount(table, instant, z, depth):
    at = instant * (depth + 2) + z
    return table[at : at + 1, :]


def curl_of_electric(ex, ey, ez, y_ex, y_ez, z_ex, z_ey):
    curl_x = (y_ez - ez) - (z_ey - ey)
    curl_y = (z_ex - ex) - (x_after(ez) - ez)
    curl_z = (x_after(ey) - ey) - (y_ex - ex)
    return curl_x, curl_y, curl_z


def curl_of_magnetic(hx, hy, hz, y_hx, y_hz, z_hx, z_hy):
    back_x = (hz - y_hz) - (hy - z_hy)
    back_y = (hx - z_hx) - (hz - x_before(hz))
    back_z = (hy - x_before(hy)) - (hx - y_hx)
    return back_x, back_y, back_z


def alone_planes(depth, instant):
    every = list(range(depth))
    left = HALO - 1 - instant
    if left == 0:
        return [depth - 1], []
    if left == 1:
        return sorted({0, depth - 2, depth - 1} & set(every)), sorted({0, depth - 1})
    return every, every


def alone_rolled(main, instant, depth, magnetic):
    planes = alone_planes(depth, instant)[0 if magnetic else 1]
    one, two, by = (0, 2, -1) if magnetic else (3, 5, 1)
    return {p: (turn(main[one, p], by, 1), turn(main[two, p], by, 1)) for p in planes}


def alone_magnetic(main, instant, depth, rolled):
    for p in alone_planes(depth, instant)[0]:
        ex, ey, ez = main[0, p], main[1, p], main[2, p]
        zero = jnp.zeros_like(ex)
        z_ex, z_ey = (main[0, p + 1], main[1, p + 1]) if p + 1 < depth else (zero, zero)
        curl = curl_of_electric(ex, ey, ez, *rolled[p], z_ex, z_ey)
        for c in range(2 if instant == HALO - 1 else 3):
            main[3 + c, p] = main[3 + c, p] - curl[c]


def alone_electric(main, instant, depth, rolled, coef, source):
    for p in alone_planes(depth, instant)[1]:
        hx, hy, hz = main[3, p], main[4, p], main[5, p]
        zero = jnp.zeros_like(hx)
        z_hx, z_hy = (main[3, p - 1], main[4, p - 1]) if p > 0 else (zero, zero)
        back = curl_of_magnetic(hx, hy, hz, *rolled[p], z_hx, z_hy)
        here = coef(p)
        main[0, p] = main[0, p] + here * (back[0] + source(p))
        main[1, p] = main[1, p] + here * back[1]
        main[2, p] = main[2, p] + here * back[2]


def interior_kernel(
    fields, material, profile, scalars, plane, coef, to_a, to_b, y_out, table
):
    depth, rows, lanes = material.shape
    eps = lambda index: scalars[HALO + index : HALO + index + 1, :]
    lane = lane_ids((1, lanes))
    there = plane[...] - lax.axis_index("gz") * depth
    inside = jnp.logical_and(there >= 0, there < depth)
    groups = [jnp.full((1, lanes), z, jnp.int32) for z in range(depth)]
    groups += [lane // WIDE, lane // GROUP - BEYOND]
    for instant in range(HALO):
        amount = jnp.where(inside, scalars[instant : instant + 1, :], 0.0)
        for index, group in enumerate(groups):
            at = instant * len(groups) + index
            table[at : at + 1, :] = jnp.where(group == there, amount, 0.0)
    base = HALO * len(groups)
    count = scalars.shape[0] - HALO
    table[base : base + count, :] = scalars[HALO : HALO + count, :]
    for z in range(depth):
        coef[z] = coef_of(material[z], eps, count)

    even = is_even("gz")

    places, end = early_rows(rows)

    def send(at, upward, downward):
        here = slice(at, at + upward.shape[0])
        if at < to_a.shape[0]:
            to_a[here, :] = jnp.where(even, upward, downward)
        if at < to_b.shape[0]:
            to_b[here, :] = jnp.where(even, downward, upward)

    for beyond in range(BEYOND):
        send(end + rows * beyond, coef[depth - 1 - beyond], coef[beyond])
    for at in range(0, rows, TILE):
        here = pl.ds(at, TILE)

        def slab(c, z):
            if c < 6:
                return fields[c, z, here, :] * slab_scale(c)
            return coef[z, here, :] if c == 6 else profile[here, :]

        low, high = y_pack_tile(slab, depth, lanes)
        y_place(y_out, at, low, high, lax.axis_size("gy") == 2)
    main = {(c, z): fields[c, z] * slab_scale(c) for c in range(6) for z in range(depth)}
    for instant in range(HALO):
        alone_magnetic(main, instant, depth, alone_rolled(main, instant, depth, True))
        for c in range(2):
            at, low, high = places[2 * instant + c]
            send(at, main[3 + c, depth - 1][low:high], main[c, 0][low:high])
        if instant < HALO - 1:
            alone_electric(
                main,
                instant,
                depth,
                alone_rolled(main, instant, depth, False),
                lambda p: coef[p],
                lambda p: plane_amount(table, instant, p, depth) * profile[...],
            )


def own_strips_kernel(fields, coef, profile, halo, strips):
    depth, rows, lanes = coef.shape
    for at in range(0, rows + TILE, TILE):
        here = pl.ds(at, TILE)
        lane = lane_ids((TILE, lanes))
        part = lax.rem(lane, WIDE) // HALO
        on_right = jnp.logical_or(part == 1, part == 2)
        for c in range(8):
            out = jnp.zeros((TILE, lanes), F32)
            for z in range(depth):
                if at == rows:
                    value = halo[depth * c + z] if c < 7 else halo[7 * depth]
                elif c < 6:
                    value = fields[c, z, here, :] * slab_scale(c)
                else:
                    value = coef[z, here, :] if c == 6 else profile[here, :]
                first = WIDE * z + HALO
                both = jnp.where(on_right, turn(value, first + 2 * HALO, 1), turn(value, first + 4 * HALO, 1))
                out = jnp.where(lane // WIDE == z, both, out)
            strips[c, here, :] = out


def frame_kernel(
    fields, coef, profile, table, halo, own, from_one, from_two, strips, to_a, to_b
):
    depth, rows, lanes = coef.shape
    wide = rows + TILE
    shape = (wide, lanes)
    lane = lane_ids(shape)
    quad = lane // HALO
    part = lax.rem(quad, WIDE // HALO)
    if lax.axis_size("gy") == 2:
        from_right, from_left = from_one[...], from_two[...]
    else:
        even = is_even("gy")
        from_right = jnp.where(even, from_one[...], from_two[...])
        from_left = jnp.where(even, from_two[...], from_one[...])
    from_left = turn(from_left, 2 * HALO, 1)
    is_halo = jnp.logical_or(part == 3, part == 4)
    mixed = (
        jnp.where(lax.rem(quad, 2) == 0, from_right, from_left),
        jnp.where(lax.rem(quad, 2) == 0, from_left, from_right),
    )
    strip = []
    for c in range(8):
        value = jnp.where(is_halo, turn(mixed[c % 2], 3 * HALO - HALO * c, 1), own[c])
        strips[c] = value
        strip.append(value)
    last, first = pl.ds(rows - TILE, TILE), pl.ds(0, TILE)
    around = lambda low, tile, high: jnp.concatenate([low, tile, high], axis=0)
    main = {}
    for z in range(depth):
        for c in range(6):
            scale = slab_scale(c)
            main[c, z] = around(fields[c, z, last, :] * scale, halo[depth * c + z], fields[c, z, first, :] * scale)
    cells = [around(coef[z, last, :], halo[6 * depth + z], coef[z, first, :]) for z in range(depth)]
    cells.append(around(profile[last, :], halo[7 * depth], profile[first, :]))

    even = is_even("gz")
    bottom, top = lane < WIDE, lane >= WIDE * (depth - 1)
    upward = jnp.zeros(shape, F32)
    downward = jnp.zeros(shape, F32)

    for instant in range(HALO):
        ex, ey, ez = strip[0:3]
        z_ex = jnp.where(top, 0.0, turn(ex, -WIDE, 1))
        z_ey = jnp.where(top, 0.0, turn(ey, -WIDE, 1))
        y_ex, y_ez = turn(ex, -1, 1), turn(ez, -1, 1)
        rolled = alone_rolled(main, instant, depth, True)
        curl = curl_of_electric(ex, ey, ez, y_ex, y_ez, z_ex, z_ey)
        for c in range(2 if instant == HALO - 1 else 3):
            strip[3 + c] = strip[3 + c] - curl[c]
        alone_magnetic(main, instant, depth, rolled)
        for c in range(2):
            item = 2 * instant + c
            rows_at = wide + TILE * item
            ups = main[3 + c, depth - 1]
            downs = main[c, 0]
            for part_at, up_at, down_at in (
                (rows_at, TILE - instant - 1, TILE - instant),
                (rows_at + HALO, TILE + HALO + instant + 1, TILE + HALO + instant),
            ):
                up = ups[up_at : up_at + HALO, :]
                down = downs[down_at : down_at + HALO, :]
                to_a[part_at : part_at + HALO, :] = jnp.where(even, up, down)
                to_b[part_at : part_at + HALO, :] = jnp.where(even, down, up)
        electric = strip[0:3]
        if instant < HALO - 1:
            hx, hy, hz = strip[3:6]
            z_hx = jnp.where(bottom, 0.0, turn(hx, WIDE, 1))
            z_hy = jnp.where(bottom, 0.0, turn(hy, WIDE, 1))
            y_hx, y_hz = turn(hx, 1, 1), turn(hz, 1, 1)
            rolled = alone_rolled(main, instant, depth, False)
            back = curl_of_magnetic(hx, hy, hz, y_hx, y_hz, z_hx, z_hy)
            amount = plane_amount(table, instant, depth, depth)
            strip[0] = strip[0] + strip[6] * (back[0] + amount * strip[7])
            strip[1] = strip[1] + strip[6] * back[1]
            strip[2] = strip[2] + strip[6] * back[2]
            alone_electric(
                main,
                instant,
                depth,
                rolled,
                lambda p: cells[p],
                lambda p: plane_amount(table, instant, p, depth) * cells[depth],
            )
        for c in range(2):
            item = 2 * instant + c
            here = lane // GROUP == item
            upward = jnp.where(here, turn(strip[3 + c], GROUP * item - WIDE * (depth - 1) - TILE, 1), upward)
            downward = jnp.where(here, turn(electric[c], GROUP * item - TILE, 1), downward)
    to_a[0:wide, :] = jnp.where(even, upward, downward)
    to_b[0:wide, :] = jnp.where(even, downward, upward)
    def send(at, up, down):
        if at < to_a.shape[0]:
            to_a[at : at + TILE, :] = jnp.where(even, up, down)
        if at < to_b.shape[0]:
            to_b[at : at + TILE, :] = jnp.where(even, down, up)

    at = wide + TILE * TRACES
    for beyond in range(BEYOND):
        send(at, halo[6 * depth + depth - 1 - beyond], halo[6 * depth + beyond])
        at += TILE
    side = lanes // (BEYOND * GROUP)
    tile_lane = lane_ids((TILE, lanes))
    for begin in range(0, wide // TILE, side):
        up = jnp.zeros((TILE, lanes), F32)
        down = jnp.zeros((TILE, lanes), F32)
        for tile in range(begin, min(begin + side, wide // TILE)):
            value = strips[6, TILE * tile : TILE * (tile + 1), :]
            for beyond in range(BEYOND):
                goal = GROUP * (BEYOND * (tile - begin) + beyond)
                here = tile_lane // GROUP == goal // GROUP
                z = depth - BEYOND + beyond
                up = jnp.where(here, turn(value, goal - WIDE * z - TILE, 1), up)
                down = jnp.where(here, turn(value, goal - WIDE * beyond - TILE, 1), down)
        send(at, up, down)
        at += TILE


def received(a, b, above, here):
    even = is_even("gz")
    one, two = (a, b) if above else (b, a)
    place = lax.axis_index("gz")
    exists = place < lax.axis_size("gz") - 1 if above else place > 0
    return jnp.where(exists, jnp.where(even, one[here], two[here]), 0.0)


def coef_beyond(a, b, above, p, depth, table, shape):
    size = lax.axis_size("gz")
    first, end = pillars(depth, size)
    z = lax.axis_index("gz") * depth + p - BEYOND
    base = HALO * (depth + 2)
    quarter = COURANT * COURANT
    low, high = quarter / table[base + 1 : base + 2, :], quarter / table[base : base + 1, :]
    layer = jnp.broadcast_to(jnp.where(z < first, low, high), shape)
    one = layer if a is None else a()
    two = layer if b is None else b()
    even = is_even("gz")
    value = jnp.where(even, one, two) if above else jnp.where(even, two, one)
    return jnp.where(jnp.logical_and(z >= 0, z < depth * size), value, 0.0)


def edges_after(ex_shifted, ez, lane):
    return jnp.where(lax.rem(lane, GROUP) == HALO - 1, ex_shifted, ez)


def edges_before(hx_shifted, hz, lane):
    return jnp.where(lax.rem(lane, GROUP) == 3 * HALO, hx_shifted, hz)


def arrived_kernel(*refs):
    pass


def prepare_kernel(wide_strips, early, strips, out):
    _, wide, lanes = wide_strips.shape
    depth = lanes // WIDE
    lane = lane_ids((TILE, lanes))
    for at in range(0, wide, TILE):
        here = pl.ds(at, TILE)
        for c in range(8):
            value = wide_strips[c, here, :]
            moved = jnp.zeros((TILE, lanes), F32)
            for z in range(depth):
                goal = GROUP * (z + BEYOND)
                moved = jnp.where(lane // GROUP == z + BEYOND, turn(value, goal - WIDE * z - TILE, 1), moved)
            strips[c, here, :] = moved


def window_kernel(
    fields,
    coef,
    profile,
    halo,
    table,
    strips,
    early_a,
    early_b,
    late_a,
    late_b,
    forward,
    material,
    fields_out,
    eps_grad,
    results,
    grad,
    sems,
    *beside,
):
    depth, rows, lanes = material.shape
    wide = rows + TILE
    shape = (wide, lanes)
    own = range(BEYOND, BEYOND + depth)
    first, last = own[0], own[-1]
    lane = lane_ids(shape)
    group = lane // GROUP

    late_strips = [received(late_a, late_b, above, slice(0, wide)) for above in (False, True)]
    places, early_end = early_rows(rows)
    traces = {}

    def merge(above, item):
        lost = item // 2 if above else item // 2 + 1
        whole = beside[TRACES * above + item]
        at, low, high = places[item]
        whole[low:high, :] = received(early_a, early_b, above, slice(at, at + high - low))
        at = wide + TILE * item
        right = received(late_a, late_b, above, slice(at, at + HALO))
        left = received(late_a, late_b, above, slice(at + HALO, at + TILE))
        whole[rows - lost : rows - lost + HALO, :] = right
        if lost < HALO:
            whole[rows + HALO + lost : wide, :] = left[0 : HALO - lost]
        if lost > 0:
            whole[0:lost, :] = left[HALO - lost : HALO]
        value = whole[...]
        if lost > 0:
            edge = turn(late_strips[above], lanes - HALO - GROUP * item, 1)
            value = jnp.where(lane >= lanes - lost, edge, value)
        lost_left = lost if above else lost - 1
        if lost_left > 0:
            edge = turn(late_strips[above], -(GROUP * item + 3 * HALO), 1)
            value = jnp.where(lane < lost_left, edge, value)
        traces[above, item] = value

    def trace(above, item):
        return traces[above, item]

    def strip_neighbours(above, item, one, two):
        goal = last if above else first - 1
        moved = turn(late_strips[above], GROUP * (goal - item), 1)
        at_goal, at_next = group == goal, group == goal + 1
        by = -GROUP if above else GROUP
        if above:
            one = turn(one, by, 1)
            two = turn(jnp.where(at_next, two + moved, two), by, 1)
            return jnp.where(at_goal, one + moved, one), two
        one = turn(jnp.where(at_goal, one + moved, one), by, 1)
        two = turn(two, by, 1)
        return one, jnp.where(at_next, two + moved, two)

    at = wide + TILE * TRACES
    lates = [late if late.shape[0] > at else None for late in (late_a, late_b)]
    joined = lambda top, tile: jnp.concatenate([top, tile], axis=0)
    zero = jnp.zeros(shape, F32)

    def late_tile(here, shift=0):
        return [None if late is None else (lambda late=late: turn(late[here], shift, 1)) for late in lates]

    wide_coef = {first + z: joined(coef[z], halo[6 * depth + z]) for z in range(depth)}
    for beyond in range(BEYOND):
        for above in (False, True):
            p = last + 1 + beyond if above else first - 1 - beyond
            from_early = slice(early_end + rows * beyond, early_end + rows * (beyond + 1))
            parts = [
                None if early.shape[0] == early_end else (lambda early=early: early[from_early])
                for early in (early_a, early_b)
            ]
            top = coef_beyond(*parts, above, p, depth, table, (rows, lanes))
            parts = late_tile(slice(at, at + TILE))
            wide_coef[p] = joined(top, coef_beyond(*parts, above, p, depth, table, (TILE, lanes)))
        at += TILE
    side = lanes // (BEYOND * GROUP)
    tile_group = lane_ids((TILE, lanes)) // GROUP
    tiles = []
    for tile in range(wide // TILE):
        here = slice(at + TILE * (tile // side), at + TILE * (tile // side) + TILE)
        start = BEYOND * GROUP * (tile % side)
        value = strips[6, TILE * tile : TILE * (tile + 1), :]
        low = coef_beyond(*late_tile(here, -start), False, tile_group, depth, table, (TILE, lanes))
        parts = late_tile(here, GROUP * (last + 1) - start)
        high = coef_beyond(*parts, True, tile_group, depth, table, (TILE, lanes))
        value = jnp.where(tile_group < first, low, value)
        tiles.append(jnp.where(tile_group > last, high, value))
    strip_coef = jnp.concatenate(tiles, axis=0)
    wide_profile = joined(profile[...], halo[7 * depth])
    strip = [strips[c] for c in range(6)]
    main = {}
    for c in range(6):
        for p in range(first - BEYOND, last + BEYOND + 1):
            z = p - first
            main[c, p] = joined(fields[c, z], halo[depth * c + z]) if first <= p <= last else zero
            if 3 <= c and first <= p <= last:
                main[c, p] = joined(fields[c, z] * slab_scale(c), halo[depth * c + z])
    below_factor = jnp.where(lax.axis_index("gz") > 0, 1.0, 0.0)
    strip_factor = jnp.where(group < first, below_factor, 1.0)

    copies = []

    def hand_out(source, target):
        copy = pltpu.make_async_copy(source, target, sems.at[len(copies)])
        copy.start()
        copies.append(copy)

    def magnetic_planes(instant):
        above = min(instant, HALO - 1 - instant, BEYOND - 1)
        return list(range(first - min(instant + 1, HALO - instant, BEYOND), last + above + 1))

    def electric_planes(instant):
        reach = min(instant + 1, HALO - 1 - instant, BEYOND)
        return list(range(first - reach, last + reach + 1))

    def in_groups(planes):
        size = -(-len(planes) // GROUPS)
        return [planes[at : at + size] for at in range(0, len(planes), size)]

    def rolled_after(mixed, planes):
        edge = {p: turn(mixed, -(GROUP * p + HALO), 1) for p in planes}
        ex = {p: turn(main[0, p], -1, 1) for p in planes}
        ez = {p: turn(jnp.where(lane == 0, edge[p], main[2, p]), -1, 1) for p in planes}
        return {p: (jnp.where(lane == lanes - 1, edge[p], ex[p]), ez[p]) for p in planes}

    def rolled_before(mixed, planes):
        edge = {p: turn(mixed, -(GROUP * p + 3 * HALO), 1) for p in planes}
        hx = {p: turn(main[3, p], 1, 1) for p in planes}
        hz = {p: turn(jnp.where(lane == lanes - 1, edge[p], main[5, p]), 1, 1) for p in planes}
        return {p: (jnp.where(lane == 0, edge[p], hx[p]), hz[p]) for p in planes}

    def strip_magnetic(instant):
        ex, ey, ez = strip[0:3]
        curl = curl_of_electric(ex, ey, ez, *strip_shifts)
        for c in range(3):
            strip[3 + c] = strip[3 + c] - strip_factor * curl[c]
        hx, hy, hz = strip[3:6]
        y_hx, y_hz = turn(hx, 1, 1), turn(hz, 1, 1)
        z_hx, z_hy = strip_neighbours(False, 2 * instant, hx, hy)
        return (y_hx, y_hz, z_hx, z_hy), edges_before(y_hx, hz, lane)

    def strip_shifted_electric(instant):
        ex, ey, ez = strip[0:3]
        y_ex, y_ez = turn(ex, -1, 1), turn(ez, -1, 1)
        z_ex, z_ey = strip_neighbours(True, 2 * instant, ex, ey)
        return (y_ex, y_ez, z_ex, z_ey), edges_after(y_ex, ez, lane)

    def strip_electric(instant):
        back = curl_of_magnetic(*strip[3:6], *strip_shifts)
        amount = plane_amount(table, instant, depth + 1, depth)
        strip[0] = strip[0] + strip_coef * (back[0] + amount * strips[7])
        strip[1] = strip[1] + strip_coef * back[1]
        strip[2] = strip[2] + strip_coef * back[2]
        return strip_shifted_electric(instant + 1)

    total = [None] * depth
    merge(True, 0)
    merge(True, 1)
    strip_shifts, mixed = strip_shifted_electric(0)
    moved = rolled_after(mixed, list(own))
    strip_shifts, mixed = strip_magnetic(0)
    for instant in range(HALO):
        item = 2 * instant
        final = instant == HALO - 1

        mixed_now = mixed
        if not final:
            strip_shifts, mixed = strip_electric(instant)
        merge(False, item)
        merge(False, item + 1)
        following = electric_planes(instant)
        later = {p: (zero, zero) for p in following}
        for planes in in_groups(magnetic_planes(instant)):
            for p in planes:
                z_ex, z_ey = main[0, p + 1], main[1, p + 1]
                if p == last:
                    z_ex, z_ey = z_ex + trace(True, item), z_ey + trace(True, item + 1)
                curl = curl_of_electric(
                    main[0, p], main[1, p], main[2, p], *moved.get(p, (zero, zero)), z_ex, z_ey
                )
                for c in range(3):
                    main[3 + c, p] = main[3 + c, p] - (curl[c] if p >= first else below_factor * curl[c])
                    if final and first <= p <= last:
                        results[3 + c, p - first] = main[3 + c, p][0:rows] * COURANT
                if final and first <= p <= last:
                    z = p - first
                    hand_out(results.at[pl.ds(3, 3), z], fields_out.at[pl.ds(3, 3), z])
            later.update(rolled_before(mixed_now, [p for p in planes if p in following]))
        moved = later

        mixed_now = mixed
        if not final:
            strip_shifts, mixed = strip_magnetic(instant + 1)
            merge(True, item + 2)
            merge(True, item + 3)
        following = [] if final else magnetic_planes(instant + 1)
        later = {}
        for planes in in_groups(electric_planes(instant)):
            for p in planes:
                z_hx, z_hy = main.get((3, p - 1), zero), main.get((4, p - 1), zero)
                if p == first:
                    z_hx, z_hy = z_hx + trace(False, item), z_hy + trace(False, item + 1)
                back = curl_of_magnetic(main[3, p], main[4, p], main[5, p], *moved[p], z_hx, z_hy)
                here = wide_coef[p]
                inside = first <= p <= last
                z = p - first
                if inside:
                    push = plane_amount(table, instant, z, depth) * wide_profile
                    back = (back[0] + push, back[1], back[2])
                for c in range(3):
                    main[c, p] = main[c, p] + here * back[c]
                    if inside:
                        term = forward[instant, c, z].astype(F32) * main[c, p][0:rows]
                        total[z] = term if total[z] is None else total[z] + term
                if inside and final:
                    for c in range(3):
                        results[c, z] = main[c, p][0:rows]
                    grad[z] = jnp.where(material[z] >= 2, -total[z], 0.0)
                    hand_out(results.at[pl.ds(0, 3), z], fields_out.at[pl.ds(0, 3), z])
                    hand_out(grad.at[z], eps_grad.at[z])
            later.update(rolled_after(mixed_now, [p for p in planes if p in following]))
        moved = later
    for copy in copies:
        copy.wait()


VMEM = pl.BlockSpec(memory_space=pltpu.VMEM)
FAR = pl.BlockSpec(memory_space=pltpu.HBM)


def near(array):
    return pltpu.with_memory_space_constraint(array, pltpu.VMEM)


def far_off(array):
    return pltpu.with_memory_space_constraint(array, pltpu.HBM), FAR


def call(kernel, operands, outs, scratch=(), far=0, aliases=None, name=None, cost=None):
    specs, arrays = [], []
    for operand in operands:
        if isinstance(operand, tuple):
            specs.append(operand[1])
            arrays.append(operand[0])
        else:
            specs.append(VMEM)
            arrays.append(near(operand))
    return pl.pallas_call(
        kernel,
        out_shape=[jax.ShapeDtypeStruct(s, F32) for s in outs[:far]] + [
            pltpu.VMEM(getattr(s, "shape", s), getattr(s, "dtype", F32)) for s in outs[far:]
        ],
        in_specs=specs,
        out_specs=[FAR] * far + [VMEM] * (len(outs) - far),
        scratch_shapes=[s if not isinstance(s, tuple) else pltpu.VMEM(s, F32) for s in scratch],
        input_output_aliases=aliases or {},
        compiler_params=pltpu.CompilerParams(vmem_limit_bytes=32 * 1024 * 1024),
        cost_estimate=cost,
        name=name,
    )(*arrays)


def on_device(
    fields_in, material, material_eps, source_plane, source_wave, source_profile, forward_fields
):
    depth, rows, lanes = material.shape
    assert source_wave.shape[0] == HALO and depth * WIDE == lanes and BEYOND <= depth
    assert (depth + 2 * BEYOND) * GROUP == lanes and TRACES * GROUP == lanes
    wide = rows + TILE
    slabs = 7 * depth + 1
    tiles = (slabs + 1) // 2

    inputs = (fields_in, material, source_profile, material_eps, source_wave)
    to_a, to_b, scalars, fields_in, material, source_profile = call(
        x_pack_kernel,
        [far_off(array) for array in inputs],
        [(tiles, TILE, lanes)] * 2
        + [(HALO + material_eps.shape[0], lanes), fields_in.shape, material, source_profile.shape],
        [
            pltpu.SMEM(material_eps.shape, F32),
            pltpu.SMEM(source_wave.shape, F32),
            pltpu.SemaphoreType.DMA((5,)),
        ],
        name="x_pack",
    )
    swap_a, swap_b = swaps(lax.axis_size("gx"), True)
    from_a = lax.ppermute(to_a, "gx", swap_a)
    from_b = lax.ppermute(to_b, "gx", swap_b)

    pairs_a, z_a, pairs_b, z_b = z_swaps(lax.axis_size("gz"), lax.axis_size("gx"))
    with_coef = [sends_coef(depth, lax.axis_size("gz"), pairs) for pairs in (pairs_a, pairs_b)]
    early_counts = [early_rows(rows)[1] + rows * BEYOND * sent for sent in with_coef]
    plane = jnp.broadcast_to(source_plane[None], (1, lanes))
    coef, early_a, early_b, partly, table = call(
        interior_kernel,
        [fields_in, material, source_profile, scalars, plane],
        [(depth, rows, lanes)]
        + [(count, lanes) for count in early_counts]
        + [(2, wide, lanes), (HALO * (depth + 2) + material_eps.shape[0], lanes)],
        name="interior",
    )
    halo, y_out = call(
        x_unpack_kernel,
        [from_a, from_b, partly],
        [(slabs, TILE, lanes), (2, wide, lanes)],
        aliases={2: 1},
        name="x_unpack",
    )
    swap_a, swap_b = swaps(lax.axis_size("gy"), True)
    if lax.axis_size("gy") == 2:
        both = lax.ppermute(y_out, "gy", swap_a)
        from_one, from_two = both[0], both[1]
    else:
        from_one = lax.ppermute(y_out[0], "gy", swap_a)
        from_two = lax.ppermute(y_out[1], "gy", swap_b)

    early_a = lax.ppermute(early_a, ("gz", "gx"), z_a)
    early_b = lax.ppermute(early_b, ("gz", "gx"), z_b)
    (own,) = call(
        own_strips_kernel,
        [fields_in, coef, source_profile, halo],
        [(8, wide, lanes)],
        name="own_strips",
    )
    side = lanes // (BEYOND * GROUP)
    coef_rows = TILE * BEYOND + TILE * (-(-wide // TILE // side))
    late_rows = [wide + TILE * TRACES + coef_rows * sent for sent in with_coef]
    strips, late_a, late_b = call(
        frame_kernel,
        [fields_in, coef, source_profile, table, halo, own, from_one, from_two],
        [(8, wide, lanes)] + [(count, lanes) for count in late_rows],
        name="frame",
    )
    late_a = lax.ppermute(late_a, ("gz", "gx"), z_a)
    late_b = lax.ppermute(late_b, ("gz", "gx"), z_b)

    (early_b,) = call(
        arrived_kernel,
        [early_b],
        [early_b.shape],
        aliases={0: 0},
        name="arrived",
        cost=pl.CostEstimate(flops=10**9, bytes_accessed=0, transcendentals=0),
    )
    strips, early_b = call(
        prepare_kernel,
        [strips, early_b],
        [(8, wide, lanes), early_b.shape],
        aliases={1: 1},
        name="prepare",
    )
    fields_out, eps_grad = call(
        window_kernel,
        [fields_in, coef, source_profile, halo, table, strips, early_a, early_b, late_a, late_b]
        + [forward_fields, material],
        [(6, depth, rows, lanes), (depth, rows, lanes)],
        [
            (6, depth, rows, lanes),
            (depth, rows, lanes),
            pltpu.SemaphoreType.DMA((3 * depth,)),
        ]
        + [(wide, lanes)] * (2 * TRACES),
        far=2,
        name="window",
    )
    return (fields_out, eps_grad)


def solution(mesh):
    placed = (
        P(None, "gz", "gx", "gy"),
        P("gz", "gx", "gy"),
        P(),
        P(),
        P(),
        P("gx", "gy"),
        P(None, None, "gz", "gx", "gy"),
    )
    return jax.shard_map(
        on_device,
        mesh=mesh,
        in_specs=placed,
        out_specs=(P(None, "gz", "gx", "gy"), P("gz", "gx", "gy")),
        check_vma=False,
    )
```

```python
import jax
import jax.numpy as jnp
from jax import lax
from jax.experimental import pallas as pl
from jax.experimental.pallas import tpu as pltpu
from jax.sharding import PartitionSpec as P

COURANT = 0.5
HALO = 4
BEYOND = 2
TILE = 8
GROUP = 16
WIDE = 32
TRACES = 2 * HALO
GROUPS = 1
F32 = jnp.float32


def lane_ids(shape):
    return lax.broadcasted_iota(jnp.int32, shape, 1)


def row_ids(shape):
    return lax.broadcasted_iota(jnp.int32, shape, 0)


def turn(value, shift, axis):
    shift = shift % value.shape[axis]
    if shift == 0:
        return value
    return pltpu.roll(value, shift, axis)


def x_after(value):
    return turn(value, -1, 0)


def x_before(value):
    return turn(value, 1, 0)


def early_rows(rows):
    places, at = [], 0
    for item in range(TRACES):
        cut = item // 2
        places.append((at, cut, rows - cut))
        at += rows - 2 * cut
    return places, at


def swaps(size, periodic):
    first = [(i, i + 1) for i in range(0, size - 1, 2)]
    second = [(i, i + 1) for i in range(1, size - 1, 2)]
    if periodic and size > 2:
        second.append((size - 1, 0))
    both = lambda pairs: pairs + [(b, a) for a, b in pairs]
    return both(first), both(second)


def z_swaps(size, beside):
    first, second = swaps(size, False)
    wide = lambda pairs: [(a * beside + i, b * beside + i) for a, b in pairs for i in range(beside)]
    idle = [z for z in range(size) if all(z != a for a, _ in second)]
    cores = [(z * beside + i, z * beside + (i ^ 1)) for z in idle for i in range(beside)]
    return first, wide(first), second, wide(second) + cores


def pillars(depth, size):
    planes = depth * size
    return planes * 3 // 8, planes * 5 // 8


def sends_coef(depth, size, pairs):
    first, end = pillars(depth, size)
    edges = [max(a, b) * depth for a, b in pairs]
    return any(edge - BEYOND < end and edge + BEYOND > first for edge in edges)


def is_even(axis):
    return lax.rem(lax.axis_index(axis), 2) == 0


def coef_of(which, eps, count):
    permit = jnp.zeros(which.shape, F32)
    for index in range(count):
        permit = jnp.where(which == index, eps(index), permit)
    return (COURANT * COURANT) / permit


def slab_scale(c):
    return 1.0 / COURANT if 3 <= c < 6 else 1.0


def x_pack_kernel(
    fields, material, profile, eps, wave, to_a, to_b, scalars, material_in, profile_in, face, eps_in, wave_in, sems
):
    depth, rows, lanes = material.shape
    pairs = [(material, material_in), (profile, profile_in), (eps, eps_in), (wave, wave_in)]
    pairs = [(fields.at[:, :, pl.ds(at, TILE), :], face.at[i]) for i, at in enumerate((0, rows - TILE))] + pairs
    copies = [pltpu.make_async_copy(one, two, sems.at[index]) for index, (one, two) in enumerate(pairs)]
    for copy in copies:
        copy.start()
    for copy in copies:
        copy.wait()
    even = is_even("gx")
    upper = row_ids((TILE, lanes)) < HALO

    def slab(side, s):
        c, z = divmod(s, depth)
        here = slice(0, TILE) if side == 0 else slice(rows - TILE, rows)
        if c < 6:
            return face[side, c, z] * slab_scale(c)
        if c == 6:
            return coef_of(material_in[z, here, :], lambda index: eps_in[index], eps.shape[0])
        return profile_in[here, :]

    count = 7 * depth + 1
    for tile in range(to_a.shape[0]):
        one, two = 2 * tile, min(2 * tile + 1, count - 1)
        left = jnp.where(upper, slab(0, one), turn(slab(0, two), HALO, 0))
        right = jnp.where(upper, turn(slab(1, one), HALO, 0), slab(1, two))
        to_a[tile] = jnp.where(even, right, left)
        to_b[tile] = jnp.where(even, left, right)
    values = [wave_in[t] * (1.0 / COURANT) for t in range(HALO)] + [eps_in[i] for i in range(eps.shape[0])]
    for index, value in enumerate(values):
        scalars[index : index + 1, :] = jnp.full((1, lanes), value)


def y_pack_tile(slab, depth, lanes):
    quad = lane_ids((TILE, lanes)) // HALO
    low = jnp.zeros((TILE, lanes), F32)
    high = jnp.zeros((TILE, lanes), F32)
    for c in range(8):
        for z in range(depth):
            value = slab(c, z)
            at = WIDE * z + HALO * c
            moved = turn(value, at, 1)
            low = jnp.where(quad == at // HALO, moved, low)
            high = jnp.where(quad == (at // HALO - 1) % (lanes // HALO), moved, high)
    return low, high


def y_place(out, at, low, high, both):
    here = pl.ds(at, TILE)
    if both:
        out[0, here, :], out[1, here, :] = low, high
    else:
        even = is_even("gy")
        out[0, here, :] = jnp.where(even, high, low)
        out[1, here, :] = jnp.where(even, low, high)


def x_unpack_kernel(from_a, from_b, partly, halo, out):
    depth = (halo.shape[0] - 1) // 7
    lanes = halo.shape[2]
    even = is_even("gx")
    upper = row_ids((TILE, lanes)) < HALO
    count = halo.shape[0]
    for tile in range(from_a.shape[0]):
        a, b = from_a[tile], from_b[tile]
        right = jnp.where(even, a, b)
        left = jnp.where(even, b, a)
        halo[2 * tile] = jnp.where(upper, right, turn(left, HALO, 0))
        if 2 * tile + 1 < count:
            halo[2 * tile + 1] = jnp.where(upper, turn(right, HALO, 0), left)
    slab = lambda c, z: halo[depth * c + z] if c < 7 else halo[7 * depth]
    low, high = y_pack_tile(slab, depth, lanes)
    y_place(out, out.shape[1] - TILE, low, high, lax.axis_size("gy") == 2)


def plane_amount(table, instant, z, depth):
    at = instant * (depth + 2) + z
    return table[at : at + 1, :]


def curl_of_electric(ex, ey, ez, y_ex, y_ez, z_ex, z_ey):
    curl_x = (y_ez - ez) - (z_ey - ey)
    curl_y = (z_ex - ex) - (x_after(ez) - ez)
    curl_z = (x_after(ey) - ey) - (y_ex - ex)
    return curl_x, curl_y, curl_z


def curl_of_magnetic(hx, hy, hz, y_hx, y_hz, z_hx, z_hy):
    back_x = (hz - y_hz) - (hy - z_hy)
    back_y = (hx - z_hx) - (hz - x_before(hz))
    back_z = (hy - x_before(hy)) - (hx - y_hx)
    return back_x, back_y, back_z


def alone_planes(depth, instant):
    every = list(range(depth))
    left = HALO - 1 - instant
    if left == 0:
        return [depth - 1], []
    if left == 1:
        return sorted({0, depth - 2, depth - 1} & set(every)), sorted({0, depth - 1})
    return every, every


def alone_rolled(main, instant, depth, magnetic):
    planes = alone_planes(depth, instant)[0 if magnetic else 1]
    one, two, by = (0, 2, -1) if magnetic else (3, 5, 1)
    return {p: (turn(main[one, p], by, 1), turn(main[two, p], by, 1)) for p in planes}


def alone_magnetic(main, instant, depth, rolled):
    for p in alone_planes(depth, instant)[0]:
        ex, ey, ez = main[0, p], main[1, p], main[2, p]
        zero = jnp.zeros_like(ex)
        z_ex, z_ey = (main[0, p + 1], main[1, p + 1]) if p + 1 < depth else (zero, zero)
        curl = curl_of_electric(ex, ey, ez, *rolled[p], z_ex, z_ey)
        for c in range(2 if instant == HALO - 1 else 3):
            main[3 + c, p] = main[3 + c, p] - curl[c]


def alone_electric(main, instant, depth, rolled, coef, source):
    for p in alone_planes(depth, instant)[1]:
        hx, hy, hz = main[3, p], main[4, p], main[5, p]
        zero = jnp.zeros_like(hx)
        z_hx, z_hy = (main[3, p - 1], main[4, p - 1]) if p > 0 else (zero, zero)
        back = curl_of_magnetic(hx, hy, hz, *rolled[p], z_hx, z_hy)
        here = coef(p)
        main[0, p] = main[0, p] + here * (back[0] + source(p))
        main[1, p] = main[1, p] + here * back[1]
        main[2, p] = main[2, p] + here * back[2]


def interior_kernel(
    fields, material, profile, scalars, plane, coef, to_a, to_b, y_out, table
):
    depth, rows, lanes = material.shape
    eps = lambda index: scalars[HALO + index : HALO + index + 1, :]
    lane = lane_ids((1, lanes))
    there = plane[...] - lax.axis_index("gz") * depth
    inside = jnp.logical_and(there >= 0, there < depth)
    groups = [jnp.full((1, lanes), z, jnp.int32) for z in range(depth)]
    groups += [lane // WIDE, lane // GROUP - BEYOND]
    for instant in range(HALO):
        amount = jnp.where(inside, scalars[instant : instant + 1, :], 0.0)
        for index, group in enumerate(groups):
            at = instant * len(groups) + index
            table[at : at + 1, :] = jnp.where(group == there, amount, 0.0)
    base = HALO * len(groups)
    count = scalars.shape[0] - HALO
    table[base : base + count, :] = scalars[HALO : HALO + count, :]
    for z in range(depth):
        coef[z] = coef_of(material[z], eps, count)

    even = is_even("gz")

    places, end = early_rows(rows)

    def send(at, upward, downward):
        here = slice(at, at + upward.shape[0])
        if at < to_a.shape[0]:
            to_a[here, :] = jnp.where(even, upward, downward)
        if at < to_b.shape[0]:
            to_b[here, :] = jnp.where(even, downward, upward)

    for beyond in range(BEYOND):
        send(end + rows * beyond, coef[depth - 1 - beyond], coef[beyond])
    for at in range(0, rows, TILE):
        here = pl.ds(at, TILE)

        def slab(c, z):
            if c < 6:
                return fields[c, z, here, :] * slab_scale(c)
            return coef[z, here, :] if c == 6 else profile[here, :]

        low, high = y_pack_tile(slab, depth, lanes)
        y_place(y_out, at, low, high, lax.axis_size("gy") == 2)
    main = {(c, z): fields[c, z] * slab_scale(c) for c in range(6) for z in range(depth)}
    for instant in range(HALO):
        alone_magnetic(main, instant, depth, alone_rolled(main, instant, depth, True))
        for c in range(2):
            at, low, high = places[2 * instant + c]
            send(at, main[3 + c, depth - 1][low:high], main[c, 0][low:high])
        if instant < HALO - 1:
            alone_electric(
                main,
                instant,
                depth,
                alone_rolled(main, instant, depth, False),
                lambda p: coef[p],
                lambda p: plane_amount(table, instant, p, depth) * profile[...],
            )


def own_strips_kernel(fields, coef, profile, halo, strips):
    depth, rows, lanes = coef.shape
    for at in range(0, rows + TILE, TILE):
        here = pl.ds(at, TILE)
        lane = lane_ids((TILE, lanes))
        part = lax.rem(lane, WIDE) // HALO
        on_right = jnp.logical_or(part == 1, part == 2)
        for c in range(8):
            out = jnp.zeros((TILE, lanes), F32)
            for z in range(depth):
                if at == rows:
                    value = halo[depth * c + z] if c < 7 else halo[7 * depth]
                elif c < 6:
                    value = fields[c, z, here, :] * slab_scale(c)
                else:
                    value = coef[z, here, :] if c == 6 else profile[here, :]
                first = WIDE * z + HALO
                both = jnp.where(on_right, turn(value, first + 2 * HALO, 1), turn(value, first + 4 * HALO, 1))
                out = jnp.where(lane // WIDE == z, both, out)
            strips[c, here, :] = out


def frame_kernel(
    fields, coef, profile, table, halo, own, from_one, from_two, strips, to_a, to_b
):
    depth, rows, lanes = coef.shape
    wide = rows + TILE
    shape = (wide, lanes)
    lane = lane_ids(shape)
    quad = lane // HALO
    part = lax.rem(quad, WIDE // HALO)
    if lax.axis_size("gy") == 2:
        from_right, from_left = from_one[...], from_two[...]
    else:
        even = is_even("gy")
        from_right = jnp.where(even, from_one[...], from_two[...])
        from_left = jnp.where(even, from_two[...], from_one[...])
    from_left = turn(from_left, 2 * HALO, 1)
    is_halo = jnp.logical_or(part == 3, part == 4)
    mixed = (
        jnp.where(lax.rem(quad, 2) == 0, from_right, from_left),
        jnp.where(lax.rem(quad, 2) == 0, from_left, from_right),
    )
    strip = []
    for c in range(8):
        value = jnp.where(is_halo, turn(mixed[c % 2], 3 * HALO - HALO * c, 1), own[c])
        strips[c] = value
        strip.append(value)
    last, first = pl.ds(rows - TILE, TILE), pl.ds(0, TILE)
    around = lambda low, tile, high: jnp.concatenate([low, tile, high], axis=0)
    main = {}
    for z in range(depth):
        for c in range(6):
            scale = slab_scale(c)
            main[c, z] = around(fields[c, z, last, :] * scale, halo[depth * c + z], fields[c, z, first, :] * scale)
    cells = [around(coef[z, last, :], halo[6 * depth + z], coef[z, first, :]) for z in range(depth)]
    cells.append(around(profile[last, :], halo[7 * depth], profile[first, :]))

    even = is_even("gz")
    bottom, top = lane < WIDE, lane >= WIDE * (depth - 1)
    upward = jnp.zeros(shape, F32)
    downward = jnp.zeros(shape, F32)

    for instant in range(HALO):
        ex, ey, ez = strip[0:3]
        z_ex = jnp.where(top, 0.0, turn(ex, -WIDE, 1))
        z_ey = jnp.where(top, 0.0, turn(ey, -WIDE, 1))
        y_ex, y_ez = turn(ex, -1, 1), turn(ez, -1, 1)
        rolled = alone_rolled(main, instant, depth, True)
        curl = curl_of_electric(ex, ey, ez, y_ex, y_ez, z_ex, z_ey)
        for c in range(2 if instant == HALO - 1 else 3):
            strip[3 + c] = strip[3 + c] - curl[c]
        alone_magnetic(main, instant, depth, rolled)
        for c in range(2):
            item = 2 * instant + c
            rows_at = wide + TILE * item
            ups = main[3 + c, depth - 1]
            downs = main[c, 0]
            for part_at, up_at, down_at in (
                (rows_at, TILE - instant - 1, TILE - instant),
                (rows_at + HALO, TILE + HALO + instant + 1, TILE + HALO + instant),
            ):
                up = ups[up_at : up_at + HALO, :]
                down = downs[down_at : down_at + HALO, :]
                to_a[part_at : part_at + HALO, :] = jnp.where(even, up, down)
                to_b[part_at : part_at + HALO, :] = jnp.where(even, down, up)
        electric = strip[0:3]
        if instant < HALO - 1:
            hx, hy, hz = strip[3:6]
            z_hx = jnp.where(bottom, 0.0, turn(hx, WIDE, 1))
            z_hy = jnp.where(bottom, 0.0, turn(hy, WIDE, 1))
            y_hx, y_hz = turn(hx, 1, 1), turn(hz, 1, 1)
            rolled = alone_rolled(main, instant, depth, False)
            back = curl_of_magnetic(hx, hy, hz, y_hx, y_hz, z_hx, z_hy)
            amount = plane_amount(table, instant, depth, depth)
            strip[0] = strip[0] + strip[6] * (back[0] + amount * strip[7])
            strip[1] = strip[1] + strip[6] * back[1]
            strip[2] = strip[2] + strip[6] * back[2]
            alone_electric(
                main,
                instant,
                depth,
                rolled,
                lambda p: cells[p],
                lambda p: plane_amount(table, instant, p, depth) * cells[depth],
            )
        for c in range(2):
            item = 2 * instant + c
            here = lane // GROUP == item
            upward = jnp.where(here, turn(strip[3 + c], GROUP * item - WIDE * (depth - 1) - TILE, 1), upward)
            downward = jnp.where(here, turn(electric[c], GROUP * item - TILE, 1), downward)
    to_a[0:wide, :] = jnp.where(even, upward, downward)
    to_b[0:wide, :] = jnp.where(even, downward, upward)
    def send(at, up, down):
        if at < to_a.shape[0]:
            to_a[at : at + TILE, :] = jnp.where(even, up, down)
        if at < to_b.shape[0]:
            to_b[at : at + TILE, :] = jnp.where(even, down, up)

    at = wide + TILE * TRACES
    for beyond in range(BEYOND):
        send(at, halo[6 * depth + depth - 1 - beyond], halo[6 * depth + beyond])
        at += TILE
    side = lanes // (BEYOND * GROUP)
    tile_lane = lane_ids((TILE, lanes))
    for begin in range(0, wide // TILE, side):
        up = jnp.zeros((TILE, lanes), F32)
        down = jnp.zeros((TILE, lanes), F32)
        for tile in range(begin, min(begin + side, wide // TILE)):
            value = strips[6, TILE * tile : TILE * (tile + 1), :]
            for beyond in range(BEYOND):
                goal = GROUP * (BEYOND * (tile - begin) + beyond)
                here = tile_lane // GROUP == goal // GROUP
                z = depth - BEYOND + beyond
                up = jnp.where(here, turn(value, goal - WIDE * z - TILE, 1), up)
                down = jnp.where(here, turn(value, goal - WIDE * beyond - TILE, 1), down)
        send(at, up, down)
        at += TILE


def received(a, b, above, here):
    even = is_even("gz")
    one, two = (a, b) if above else (b, a)
    place = lax.axis_index("gz")
    exists = place < lax.axis_size("gz") - 1 if above else place > 0
    return jnp.where(exists, jnp.where(even, one[here], two[here]), 0.0)


def coef_beyond(a, b, above, p, depth, table, shape):
    size = lax.axis_size("gz")
    first, end = pillars(depth, size)
    z = lax.axis_index("gz") * depth + p - BEYOND
    base = HALO * (depth + 2)
    quarter = COURANT * COURANT
    low, high = quarter / table[base + 1 : base + 2, :], quarter / table[base : base + 1, :]
    layer = jnp.broadcast_to(jnp.where(z < first, low, high), shape)
    one = layer if a is None else a()
    two = layer if b is None else b()
    even = is_even("gz")
    value = jnp.where(even, one, two) if above else jnp.where(even, two, one)
    return jnp.where(jnp.logical_and(z >= 0, z < depth * size), value, 0.0)


def edges_after(ex_shifted, ez, lane):
    return jnp.where(lax.rem(lane, GROUP) == HALO - 1, ex_shifted, ez)


def edges_before(hx_shifted, hz, lane):
    return jnp.where(lax.rem(lane, GROUP) == 3 * HALO, hx_shifted, hz)


def arrived_kernel(*refs):
    pass


def rolled_after(main, mixed, planes, lane):
    end = lane.shape[1] - 1
    edge = {p: turn(mixed, -(GROUP * p + HALO), 1) for p in planes}
    ex = {p: turn(main[0, p], -1, 1) for p in planes}
    ez = {p: turn(jnp.where(lane == 0, edge[p], main[2, p]), -1, 1) for p in planes}
    return {p: (jnp.where(lane == end, edge[p], ex[p]), ez[p]) for p in planes}


def rolled_before(main, mixed, planes, lane):
    end = lane.shape[1] - 1
    edge = {p: turn(mixed, -(GROUP * p + 3 * HALO), 1) for p in planes}
    hx = {p: turn(main[3, p], 1, 1) for p in planes}
    hz = {p: turn(jnp.where(lane == end, edge[p], main[5, p]), 1, 1) for p in planes}
    return {p: (jnp.where(lane == 0, edge[p], hx[p]), hz[p]) for p in planes}


def below_factors(group):
    factor = jnp.where(lax.axis_index("gz") > 0, 1.0, 0.0)
    return factor, jnp.where(group < BEYOND, factor, 1.0)


def wide_field(fields, halo, c, z):
    depth = fields.shape[1]
    own = fields[c, z] * slab_scale(c) if c >= 3 else fields[c, z]
    return jnp.concatenate([own, halo[depth * c + z]], axis=0)


def prepare_kernel(fields, halo, wide_strips, early, strips, magnetic, shifted, out):
    _, wide, lanes = wide_strips.shape
    depth = lanes // WIDE
    first, last = BEYOND, BEYOND + depth - 1
    lane = lane_ids((TILE, lanes))
    for at in range(0, wide, TILE):
        here = pl.ds(at, TILE)
        for c in range(8):
            value = wide_strips[c, here, :]
            moved = jnp.zeros((TILE, lanes), F32)
            for z in range(depth):
                goal = GROUP * (z + BEYOND)
                moved = jnp.where(lane // GROUP == z + BEYOND, turn(value, goal - WIDE * z - TILE, 1), moved)
            strips[c, here, :] = moved
    lane = lane_ids((wide, lanes))
    below_factor, strip_factor = below_factors(lane // GROUP)
    ex, ey, ez, hx, hy, hz = [strips[c] for c in range(6)]
    y_ex, y_ez = turn(ex, -1, 1), turn(ez, -1, 1)
    curl = curl_of_electric(ex, ey, ez, y_ex, y_ez, turn(ex, -GROUP, 1), turn(ey, -GROUP, 1))
    hx, hy, hz = [value - strip_factor * curl[c] for c, value in enumerate((hx, hy, hz))]
    for c, value in enumerate((hx, hy, hz)):
        magnetic[c, depth + 1] = value
    zero = jnp.zeros((wide, lanes), F32)
    main = {(c, first + z): wide_field(fields, halo, c, z) for c in range(6) for z in range(depth)}
    for c in range(6):
        main[c, first - 1] = main[c, last + 1] = zero
    moved = rolled_after(main, edges_after(y_ex, ez, lane), range(first, last + 1), lane)
    mixed = edges_before(turn(hx, 1, 1), hz, lane)
    for p in range(first - 1, last + 1):
        curl = curl_of_electric(
            main[0, p], main[1, p], main[2, p], *moved.get(p, (zero, zero)), main[0, p + 1], main[1, p + 1]
        )
        for c in range(3):
            main[3 + c, p] = main[3 + c, p] - (curl[c] if p >= first else below_factor * curl[c])
            magnetic[c, p - first + 1] = main[3 + c, p]
    moved = rolled_before(main, mixed, range(first - 1, last), lane)
    for p in range(first - 1, last):
        shifted[0, p - first + 1], shifted[1, p - first + 1] = moved[p]


def window_kernel(
    fields,
    coef,
    profile,
    halo,
    table,
    strips,
    magnetic,
    shifted,
    early_a,
    early_b,
    late_a,
    late_b,
    forward,
    material,
    fields_out,
    eps_grad,
    results,
    grad,
    sems,
    *beside,
):
    depth, rows, lanes = material.shape
    wide = rows + TILE
    shape = (wide, lanes)
    own = range(BEYOND, BEYOND + depth)
    first, last = own[0], own[-1]
    lane = lane_ids(shape)
    group = lane // GROUP

    late_strips = [received(late_a, late_b, above, slice(0, wide)) for above in (False, True)]
    places, early_end = early_rows(rows)
    traces = {}

    def merge(above, item):
        lost = item // 2 if above else item // 2 + 1
        whole = beside[TRACES * above + item]
        at, low, high = places[item]
        whole[low:high, :] = received(early_a, early_b, above, slice(at, at + high - low))
        at = wide + TILE * item
        right = received(late_a, late_b, above, slice(at, at + HALO))
        left = received(late_a, late_b, above, slice(at + HALO, at + TILE))
        whole[rows - lost : rows - lost + HALO, :] = right
        if lost < HALO:
            whole[rows + HALO + lost : wide, :] = left[0 : HALO - lost]
        if lost > 0:
            whole[0:lost, :] = left[HALO - lost : HALO]
        value = whole[...]
        if lost > 0:
            edge = turn(late_strips[above], lanes - HALO - GROUP * item, 1)
            value = jnp.where(lane >= lanes - lost, edge, value)
        lost_left = lost if above else lost - 1
        if lost_left > 0:
            edge = turn(late_strips[above], -(GROUP * item + 3 * HALO), 1)
            value = jnp.where(lane < lost_left, edge, value)
        traces[above, item] = value

    def trace(above, item):
        return traces[above, item]

    def strip_neighbours(above, item, one, two):
        goal = last if above else first - 1
        moved = turn(late_strips[above], GROUP * (goal - item), 1)
        at_goal, at_next = group == goal, group == goal + 1
        by = -GROUP if above else GROUP
        if above:
            one = turn(one, by, 1)
            two = turn(jnp.where(at_next, two + moved, two), by, 1)
            return jnp.where(at_goal, one + moved, one), two
        one = turn(jnp.where(at_goal, one + moved, one), by, 1)
        two = turn(two, by, 1)
        return one, jnp.where(at_next, two + moved, two)

    at = wide + TILE * TRACES
    lates = [late if late.shape[0] > at else None for late in (late_a, late_b)]
    joined = lambda top, tile: jnp.concatenate([top, tile], axis=0)
    zero = jnp.zeros(shape, F32)

    def late_tile(here, shift=0):
        return [None if late is None else (lambda late=late: turn(late[here], shift, 1)) for late in lates]

    wide_coef = {first + z: joined(coef[z], halo[6 * depth + z]) for z in range(depth)}
    for beyond in range(BEYOND):
        for above in (False, True):
            p = last + 1 + beyond if above else first - 1 - beyond
            from_early = slice(early_end + rows * beyond, early_end + rows * (beyond + 1))
            parts = [
                None if early.shape[0] == early_end else (lambda early=early: early[from_early])
                for early in (early_a, early_b)
            ]
            top = coef_beyond(*parts, above, p, depth, table, (rows, lanes))
            parts = late_tile(slice(at, at + TILE))
            wide_coef[p] = joined(top, coef_beyond(*parts, above, p, depth, table, (TILE, lanes)))
        at += TILE
    side = lanes // (BEYOND * GROUP)
    tile_group = lane_ids((TILE, lanes)) // GROUP
    tiles = []
    for tile in range(wide // TILE):
        here = slice(at + TILE * (tile // side), at + TILE * (tile // side) + TILE)
        start = BEYOND * GROUP * (tile % side)
        value = strips[6, TILE * tile : TILE * (tile + 1), :]
        low = coef_beyond(*late_tile(here, -start), False, tile_group, depth, table, (TILE, lanes))
        parts = late_tile(here, GROUP * (last + 1) - start)
        high = coef_beyond(*parts, True, tile_group, depth, table, (TILE, lanes))
        value = jnp.where(tile_group < first, low, value)
        tiles.append(jnp.where(tile_group > last, high, value))
    strip_coef = jnp.concatenate(tiles, axis=0)
    wide_profile = joined(profile[...], halo[7 * depth])
    strip = [strips[c] for c in range(6)]
    main = {(c, p): zero for c in range(6) for p in range(first - BEYOND, last + BEYOND + 1)}
    for c in range(3):
        for z in range(depth):
            main[c, first + z] = wide_field(fields, halo, c, z)
        for p in range(first - 1, last + 1):
            main[3 + c, p] = magnetic[c, p - first + 1]
        strip[3 + c] = magnetic[c, depth + 1]
    below_factor, strip_factor = below_factors(group)

    copies = []

    def hand_out(source, target):
        copy = pltpu.make_async_copy(source, target, sems.at[len(copies)])
        copy.start()
        copies.append(copy)

    def magnetic_planes(instant):
        above = min(instant, HALO - 1 - instant, BEYOND - 1)
        return list(range(first - min(instant + 1, HALO - instant, BEYOND), last + above + 1))

    def electric_planes(instant):
        reach = min(instant + 1, HALO - 1 - instant, BEYOND)
        return list(range(first - reach, last + reach + 1))

    def in_groups(planes):
        size = -(-len(planes) // GROUPS)
        return [planes[at : at + size] for at in range(0, len(planes), size)]

    def strip_magnetic(instant):
        ex, ey, ez = strip[0:3]
        curl = curl_of_electric(ex, ey, ez, *strip_shifts)
        for c in range(3):
            strip[3 + c] = strip[3 + c] - strip_factor * curl[c]
        return strip_shifted_magnetic(instant)

    def strip_shifted_magnetic(instant):
        hx, hy, hz = strip[3:6]
        y_hx, y_hz = turn(hx, 1, 1), turn(hz, 1, 1)
        z_hx, z_hy = strip_neighbours(False, 2 * instant, hx, hy)
        return (y_hx, y_hz, z_hx, z_hy), edges_before(y_hx, hz, lane)

    def strip_shifted_electric(instant):
        ex, ey, ez = strip[0:3]
        y_ex, y_ez = turn(ex, -1, 1), turn(ez, -1, 1)
        z_ex, z_ey = strip_neighbours(True, 2 * instant, ex, ey)
        return (y_ex, y_ez, z_ex, z_ey), edges_after(y_ex, ez, lane)

    def strip_electric(instant):
        back = curl_of_magnetic(*strip[3:6], *strip_shifts)
        amount = plane_amount(table, instant, depth + 1, depth)
        strip[0] = strip[0] + strip_coef * (back[0] + amount * strips[7])
        strip[1] = strip[1] + strip_coef * back[1]
        strip[2] = strip[2] + strip_coef * back[2]
        return strip_shifted_electric(instant + 1)

    total = [None] * depth
    merge(True, 0)
    merge(True, 1)
    at_last = group == last
    strip[3] = jnp.where(at_last, strip[3] + turn(late_strips[True], GROUP * (last - 1), 1), strip[3])
    strip[4] = jnp.where(at_last, strip[4] - turn(late_strips[True], GROUP * last, 1), strip[4])
    main[3, last] = main[3, last] + trace(True, 1)
    main[4, last] = main[4, last] - trace(True, 0)
    strip_shifts, mixed = strip_shifted_magnetic(0)
    moved = {p: (shifted[0, p - first + 1], shifted[1, p - first + 1]) for p in range(first - 1, last)}
    moved[last + 1] = (zero, zero)
    for instant in range(HALO):
        item = 2 * instant
        final = instant == HALO - 1

        mixed_now = mixed
        if not final:
            strip_shifts, mixed = strip_electric(instant)
        merge(False, item)
        merge(False, item + 1)
        if instant == 0:
            moved.update(rolled_before(main, mixed_now, [last], lane))
        else:
            following = electric_planes(instant)
            later = {p: (zero, zero) for p in following}
            for planes in in_groups(magnetic_planes(instant)):
                for p in planes:
                    z_ex, z_ey = main[0, p + 1], main[1, p + 1]
                    if p == last:
                        z_ex, z_ey = z_ex + trace(True, item), z_ey + trace(True, item + 1)
                    curl = curl_of_electric(
                        main[0, p], main[1, p], main[2, p], *moved.get(p, (zero, zero)), z_ex, z_ey
                    )
                    for c in range(3):
                        main[3 + c, p] = main[3 + c, p] - (curl[c] if p >= first else below_factor * curl[c])
                        if final and first <= p <= last:
                            results[3 + c, p - first] = main[3 + c, p][0:rows] * COURANT
                    if final and first <= p <= last:
                        z = p - first
                        hand_out(results.at[pl.ds(3, 3), z], fields_out.at[pl.ds(3, 3), z])
                later.update(rolled_before(main, mixed_now, [p for p in planes if p in following], lane))
            moved = later

        mixed_now = mixed
        if not final:
            strip_shifts, mixed = strip_magnetic(instant + 1)
            merge(True, item + 2)
            merge(True, item + 3)
        following = [] if final else magnetic_planes(instant + 1)
        later = {}
        for planes in in_groups(electric_planes(instant)):
            for p in planes:
                z_hx, z_hy = main.get((3, p - 1), zero), main.get((4, p - 1), zero)
                if p == first:
                    z_hx, z_hy = z_hx + trace(False, item), z_hy + trace(False, item + 1)
                back = curl_of_magnetic(main[3, p], main[4, p], main[5, p], *moved[p], z_hx, z_hy)
                here = wide_coef[p]
                inside = first <= p <= last
                z = p - first
                if inside:
                    push = plane_amount(table, instant, z, depth) * wide_profile
                    back = (back[0] + push, back[1], back[2])
                for c in range(3):
                    main[c, p] = main[c, p] + here * back[c]
                    if inside:
                        term = forward[instant, c, z].astype(F32) * main[c, p][0:rows]
                        total[z] = term if total[z] is None else total[z] + term
                if inside and final:
                    for c in range(3):
                        results[c, z] = main[c, p][0:rows]
                    grad[z] = jnp.where(material[z] >= 2, -total[z], 0.0)
                    hand_out(results.at[pl.ds(0, 3), z], fields_out.at[pl.ds(0, 3), z])
                    hand_out(grad.at[z], eps_grad.at[z])
            later.update(rolled_after(main, mixed_now, [p for p in planes if p in following], lane))
        moved = later
    for copy in copies:
        copy.wait()


VMEM = pl.BlockSpec(memory_space=pltpu.VMEM)
FAR = pl.BlockSpec(memory_space=pltpu.HBM)


def near(array):
    return pltpu.with_memory_space_constraint(array, pltpu.VMEM)


def far_off(array):
    return pltpu.with_memory_space_constraint(array, pltpu.HBM), FAR


def call(kernel, operands, outs, scratch=(), far=0, aliases=None, name=None, cost=None):
    specs, arrays = [], []
    for operand in operands:
        if isinstance(operand, tuple):
            specs.append(operand[1])
            arrays.append(operand[0])
        else:
            specs.append(VMEM)
            arrays.append(near(operand))
    return pl.pallas_call(
        kernel,
        out_shape=[jax.ShapeDtypeStruct(s, F32) for s in outs[:far]] + [
            pltpu.VMEM(getattr(s, "shape", s), getattr(s, "dtype", F32)) for s in outs[far:]
        ],
        in_specs=specs,
        out_specs=[FAR] * far + [VMEM] * (len(outs) - far),
        scratch_shapes=[s if not isinstance(s, tuple) else pltpu.VMEM(s, F32) for s in scratch],
        input_output_aliases=aliases or {},
        compiler_params=pltpu.CompilerParams(vmem_limit_bytes=32 * 1024 * 1024),
        cost_estimate=cost,
        name=name,
    )(*arrays)


def on_device(
    fields_in, material, material_eps, source_plane, source_wave, source_profile, forward_fields
):
    depth, rows, lanes = material.shape
    assert source_wave.shape[0] == HALO and depth * WIDE == lanes and BEYOND <= depth
    assert (depth + 2 * BEYOND) * GROUP == lanes and TRACES * GROUP == lanes
    wide = rows + TILE
    slabs = 7 * depth + 1
    tiles = (slabs + 1) // 2

    inputs = (fields_in, material, source_profile, material_eps, source_wave)
    to_a, to_b, scalars, material, source_profile = call(
        x_pack_kernel,
        [far_off(array) for array in inputs],
        [(tiles, TILE, lanes)] * 2
        + [(HALO + material_eps.shape[0], lanes), material, source_profile.shape],
        [
            (2, 6, depth, TILE, lanes),
            pltpu.SMEM(material_eps.shape, F32),
            pltpu.SMEM(source_wave.shape, F32),
            pltpu.SemaphoreType.DMA((6,)),
        ],
        name="x_pack",
    )
    swap_a, swap_b = swaps(lax.axis_size("gx"), True)
    from_a = lax.ppermute(to_a, "gx", swap_a)
    from_b = lax.ppermute(to_b, "gx", swap_b)

    pairs_a, z_a, pairs_b, z_b = z_swaps(lax.axis_size("gz"), lax.axis_size("gx"))
    with_coef = [sends_coef(depth, lax.axis_size("gz"), pairs) for pairs in (pairs_a, pairs_b)]
    early_counts = [early_rows(rows)[1] + rows * BEYOND * sent for sent in with_coef]
    plane = jnp.broadcast_to(source_plane[None], (1, lanes))
    coef, early_a, early_b, partly, table = call(
        interior_kernel,
        [fields_in, material, source_profile, scalars, plane],
        [(depth, rows, lanes)]
        + [(count, lanes) for count in early_counts]
        + [(2, wide, lanes), (HALO * (depth + 2) + material_eps.shape[0], lanes)],
        name="interior",
    )
    halo, y_out = call(
        x_unpack_kernel,
        [from_a, from_b, partly],
        [(slabs, TILE, lanes), (2, wide, lanes)],
        aliases={2: 1},
        name="x_unpack",
    )
    swap_a, swap_b = swaps(lax.axis_size("gy"), True)
    if lax.axis_size("gy") == 2:
        both = lax.ppermute(y_out, "gy", swap_a)
        from_one, from_two = both[0], both[1]
    else:
        from_one = lax.ppermute(y_out[0], "gy", swap_a)
        from_two = lax.ppermute(y_out[1], "gy", swap_b)

    early_a = lax.ppermute(early_a, ("gz", "gx"), z_a)
    early_b = lax.ppermute(early_b, ("gz", "gx"), z_b)
    (own,) = call(
        own_strips_kernel,
        [fields_in, coef, source_profile, halo],
        [(8, wide, lanes)],
        name="own_strips",
    )
    side = lanes // (BEYOND * GROUP)
    coef_rows = TILE * BEYOND + TILE * (-(-wide // TILE // side))
    late_rows = [wide + TILE * TRACES + coef_rows * sent for sent in with_coef]
    strips, late_a, late_b = call(
        frame_kernel,
        [fields_in, coef, source_profile, table, halo, own, from_one, from_two],
        [(8, wide, lanes)] + [(count, lanes) for count in late_rows],
        name="frame",
    )
    late_a = lax.ppermute(late_a, ("gz", "gx"), z_a)
    late_b = lax.ppermute(late_b, ("gz", "gx"), z_b)

    (early_b,) = call(
        arrived_kernel,
        [early_b],
        [early_b.shape],
        aliases={0: 0},
        name="arrived",
        cost=pl.CostEstimate(flops=10**9, bytes_accessed=0, transcendentals=0),
    )
    strips, magnetic, shifted, early_b = call(
        prepare_kernel,
        [fields_in, halo, strips, early_b],
        [(8, wide, lanes), (3, depth + 2, wide, lanes), (2, depth, wide, lanes), early_b.shape],
        aliases={3: 3},
        name="prepare",
    )
    fields_out, eps_grad = call(
        window_kernel,
        [fields_in, coef, source_profile, halo, table, strips, magnetic, shifted]
        + [early_a, early_b, late_a, late_b]
        + [forward_fields, material],
        [(6, depth, rows, lanes), (depth, rows, lanes)],
        [
            (6, depth, rows, lanes),
            (depth, rows, lanes),
            pltpu.SemaphoreType.DMA((3 * depth,)),
        ]
        + [(wide, lanes)] * (2 * TRACES),
        far=2,
        name="window",
    )
    return (fields_out, eps_grad)


def solution(mesh):
    placed = (
        P(None, "gz", "gx", "gy"),
        P("gz", "gx", "gy"),
        P(),
        P(),
        P(),
        P("gx", "gy"),
        P(None, None, "gz", "gx", "gy"),
    )
    return jax.shard_map(
        on_device,
        mesh=mesh,
        in_specs=placed,
        out_specs=(P(None, "gz", "gx", "gy"), P("gz", "gx", "gy")),
        check_vma=False,
    )
```

```python
import jax
import jax.numpy as jnp
from jax import lax
from jax.experimental import pallas as pl
from jax.experimental.pallas import tpu as pltpu
from jax.sharding import PartitionSpec as P

COURANT = 0.5
HALO = 4
BEYOND = 2
TILE = 8
GROUP = 16
WIDE = 32
TRACES = 2 * HALO
GROUPS = 1
F32 = jnp.float32


def lane_ids(shape):
    return lax.broadcasted_iota(jnp.int32, shape, 1)


def row_ids(shape):
    return lax.broadcasted_iota(jnp.int32, shape, 0)


def turn(value, shift, axis):
    shift = shift % value.shape[axis]
    if shift == 0:
        return value
    return pltpu.roll(value, shift, axis)


def x_after(value):
    return turn(value, -1, 0)


def x_before(value):
    return turn(value, 1, 0)


def early_rows(rows):
    places, at = [], 0
    for item in range(TRACES):
        cut = item // 2
        places.append((at, cut, rows - cut))
        at += rows - 2 * cut
    return places, at


def swaps(size, periodic):
    first = [(i, i + 1) for i in range(0, size - 1, 2)]
    second = [(i, i + 1) for i in range(1, size - 1, 2)]
    if periodic and size > 2:
        second.append((size - 1, 0))
    both = lambda pairs: pairs + [(b, a) for a, b in pairs]
    return both(first), both(second)


def z_swaps(size, beside):
    first, second = swaps(size, False)
    wide = lambda pairs: [(a * beside + i, b * beside + i) for a, b in pairs for i in range(beside)]
    idle = [z for z in range(size) if all(z != a for a, _ in second)]
    cores = [(z * beside + i, z * beside + (i ^ 1)) for z in idle for i in range(beside)]
    return first, wide(first), second, wide(second) + cores


def pillars(depth, size):
    planes = depth * size
    return planes * 3 // 8, planes * 5 // 8


def sends_coef(depth, size, pairs):
    first, end = pillars(depth, size)
    edges = [max(a, b) * depth for a, b in pairs]
    return any(edge - BEYOND < end and edge + BEYOND > first for edge in edges)


def is_even(axis):
    return lax.rem(lax.axis_index(axis), 2) == 0


def coef_of(which, eps, count):
    permit = jnp.zeros(which.shape, F32)
    for index in range(count):
        permit = jnp.where(which == index, eps(index), permit)
    return (COURANT * COURANT) / permit


def slab_scale(c):
    return 1.0 / COURANT if 3 <= c < 6 else 1.0


def x_pack_kernel(
    fields, material, profile, eps, wave, to_a, to_b, scalars, material_in, profile_in, face, eps_in, wave_in, sems
):
    depth, rows, lanes = material.shape
    pairs = [(material, material_in), (profile, profile_in), (eps, eps_in), (wave, wave_in)]
    pairs = [(fields.at[:, :, pl.ds(at, TILE), :], face.at[i]) for i, at in enumerate((0, rows - TILE))] + pairs
    copies = [pltpu.make_async_copy(one, two, sems.at[index]) for index, (one, two) in enumerate(pairs)]
    for copy in copies:
        copy.start()
    for copy in copies:
        copy.wait()
    even = is_even("gx")
    upper = row_ids((TILE, lanes)) < HALO

    def slab(side, s):
        c, z = divmod(s, depth)
        here = slice(0, TILE) if side == 0 else slice(rows - TILE, rows)
        if c < 6:
            return face[side, c, z] * slab_scale(c)
        if c == 6:
            return coef_of(material_in[z, here, :], lambda index: eps_in[index], eps.shape[0])
        return profile_in[here, :]

    count = 7 * depth + 1
    for tile in range(to_a.shape[0]):
        one, two = 2 * tile, min(2 * tile + 1, count - 1)
        left = jnp.where(upper, slab(0, one), turn(slab(0, two), HALO, 0))
        right = jnp.where(upper, turn(slab(1, one), HALO, 0), slab(1, two))
        to_a[tile] = jnp.where(even, right, left)
        to_b[tile] = jnp.where(even, left, right)
    values = [wave_in[t] * (1.0 / COURANT) for t in range(HALO)] + [eps_in[i] for i in range(eps.shape[0])]
    for index, value in enumerate(values):
        scalars[index : index + 1, :] = jnp.full((1, lanes), value)


def y_pack_tile(slab, depth, lanes):
    quad = lane_ids((TILE, lanes)) // HALO
    low = jnp.zeros((TILE, lanes), F32)
    high = jnp.zeros((TILE, lanes), F32)
    for c in range(8):
        for z in range(depth):
            value = slab(c, z)
            at = WIDE * z + HALO * c
            moved = turn(value, at, 1)
            low = jnp.where(quad == at // HALO, moved, low)
            high = jnp.where(quad == (at // HALO - 1) % (lanes // HALO), moved, high)
    return low, high


def y_place(out, at, low, high, both):
    here = pl.ds(at, TILE)
    if both:
        out[0, here, :], out[1, here, :] = low, high
    else:
        even = is_even("gy")
        out[0, here, :] = jnp.where(even, high, low)
        out[1, here, :] = jnp.where(even, low, high)


def x_unpack_kernel(from_a, from_b, partly, halo, out):
    depth = (halo.shape[0] - 1) // 7
    lanes = halo.shape[2]
    even = is_even("gx")
    upper = row_ids((TILE, lanes)) < HALO
    count = halo.shape[0]
    for tile in range(from_a.shape[0]):
        a, b = from_a[tile], from_b[tile]
        right = jnp.where(even, a, b)
        left = jnp.where(even, b, a)
        halo[2 * tile] = jnp.where(upper, right, turn(left, HALO, 0))
        if 2 * tile + 1 < count:
            halo[2 * tile + 1] = jnp.where(upper, turn(right, HALO, 0), left)
    slab = lambda c, z: halo[depth * c + z] if c < 7 else halo[7 * depth]
    low, high = y_pack_tile(slab, depth, lanes)
    y_place(out, out.shape[1] - TILE, low, high, lax.axis_size("gy") == 2)


def plane_amount(table, instant, z, depth):
    at = instant * (depth + 2) + z
    return table[at : at + 1, :]


def curl_of_electric(ex, ey, ez, y_ex, y_ez, z_ex, z_ey):
    curl_x = (y_ez - ez) - (z_ey - ey)
    curl_y = (z_ex - ex) - (x_after(ez) - ez)
    curl_z = (x_after(ey) - ey) - (y_ex - ex)
    return curl_x, curl_y, curl_z


def curl_of_magnetic(hx, hy, hz, y_hx, y_hz, z_hx, z_hy):
    back_x = (hz - y_hz) - (hy - z_hy)
    back_y = (hx - z_hx) - (hz - x_before(hz))
    back_z = (hy - x_before(hy)) - (hx - y_hx)
    return back_x, back_y, back_z


def alone_planes(depth, instant):
    every = list(range(depth))
    left = HALO - 1 - instant
    if left == 0:
        return [depth - 1], []
    if left == 1:
        return sorted({0, depth - 2, depth - 1} & set(every)), sorted({0, depth - 1})
    return every, every


def alone_rolled(main, instant, depth, magnetic):
    planes = alone_planes(depth, instant)[0 if magnetic else 1]
    one, two, by = (0, 2, -1) if magnetic else (3, 5, 1)
    return {p: (turn(main[one, p], by, 1), turn(main[two, p], by, 1)) for p in planes}


def alone_magnetic(main, instant, depth, rolled):
    for p in alone_planes(depth, instant)[0]:
        ex, ey, ez = main[0, p], main[1, p], main[2, p]
        zero = jnp.zeros_like(ex)
        z_ex, z_ey = (main[0, p + 1], main[1, p + 1]) if p + 1 < depth else (zero, zero)
        curl = curl_of_electric(ex, ey, ez, *rolled[p], z_ex, z_ey)
        for c in range(2 if instant == HALO - 1 else 3):
            main[3 + c, p] = main[3 + c, p] - curl[c]


def alone_electric(main, instant, depth, rolled, coef, source):
    for p in alone_planes(depth, instant)[1]:
        hx, hy, hz = main[3, p], main[4, p], main[5, p]
        zero = jnp.zeros_like(hx)
        z_hx, z_hy = (main[3, p - 1], main[4, p - 1]) if p > 0 else (zero, zero)
        back = curl_of_magnetic(hx, hy, hz, *rolled[p], z_hx, z_hy)
        here = coef(p)
        main[0, p] = main[0, p] + here * (back[0] + source(p))
        main[1, p] = main[1, p] + here * back[1]
        main[2, p] = main[2, p] + here * back[2]


def interior_kernel(
    fields, material, profile, scalars, plane, coef, to_a, to_b, y_out, table
):
    depth, rows, lanes = material.shape
    eps = lambda index: scalars[HALO + index : HALO + index + 1, :]
    lane = lane_ids((1, lanes))
    there = plane[...] - lax.axis_index("gz") * depth
    inside = jnp.logical_and(there >= 0, there < depth)
    groups = [jnp.full((1, lanes), z, jnp.int32) for z in range(depth)]
    groups += [lane // WIDE, lane // GROUP - BEYOND]
    for instant in range(HALO):
        amount = jnp.where(inside, scalars[instant : instant + 1, :], 0.0)
        for index, group in enumerate(groups):
            at = instant * len(groups) + index
            table[at : at + 1, :] = jnp.where(group == there, amount, 0.0)
    base = HALO * len(groups)
    count = scalars.shape[0] - HALO
    table[base : base + count, :] = scalars[HALO : HALO + count, :]
    for z in range(depth):
        coef[z] = coef_of(material[z], eps, count)

    even = is_even("gz")

    places, end = early_rows(rows)

    def send(at, upward, downward):
        here = slice(at, at + upward.shape[0])
        if at < to_a.shape[0]:
            to_a[here, :] = jnp.where(even, upward, downward)
        if at < to_b.shape[0]:
            to_b[here, :] = jnp.where(even, downward, upward)

    for beyond in range(BEYOND):
        send(end + rows * beyond, coef[depth - 1 - beyond], coef[beyond])
    for at in range(0, rows, TILE):
        here = pl.ds(at, TILE)

        def slab(c, z):
            if c < 6:
                return fields[c, z, here, :] * slab_scale(c)
            return coef[z, here, :] if c == 6 else profile[here, :]

        low, high = y_pack_tile(slab, depth, lanes)
        y_place(y_out, at, low, high, lax.axis_size("gy") == 2)
    main = {(c, z): fields[c, z] * slab_scale(c) for c in range(6) for z in range(depth)}
    for instant in range(HALO):
        alone_magnetic(main, instant, depth, alone_rolled(main, instant, depth, True))
        for c in range(2):
            at, low, high = places[2 * instant + c]
            send(at, main[3 + c, depth - 1][low:high], main[c, 0][low:high])
        if instant < HALO - 1:
            alone_electric(
                main,
                instant,
                depth,
                alone_rolled(main, instant, depth, False),
                lambda p: coef[p],
                lambda p: plane_amount(table, instant, p, depth) * profile[...],
            )


def own_strips_kernel(fields, coef, profile, halo, strips):
    depth, rows, lanes = coef.shape
    for at in range(0, rows + TILE, TILE):
        here = pl.ds(at, TILE)
        lane = lane_ids((TILE, lanes))
        part = lax.rem(lane, WIDE) // HALO
        on_right = jnp.logical_or(part == 1, part == 2)
        for c in range(8):
            out = jnp.zeros((TILE, lanes), F32)
            for z in range(depth):
                if at == rows:
                    value = halo[depth * c + z] if c < 7 else halo[7 * depth]
                elif c < 6:
                    value = fields[c, z, here, :] * slab_scale(c)
                else:
                    value = coef[z, here, :] if c == 6 else profile[here, :]
                first = WIDE * z + HALO
                both = jnp.where(on_right, turn(value, first + 2 * HALO, 1), turn(value, first + 4 * HALO, 1))
                out = jnp.where(lane // WIDE == z, both, out)
            strips[c, here, :] = out


def frame_kernel(
    fields, coef, profile, table, halo, own, from_one, from_two, strips, to_a, to_b
):
    depth, rows, lanes = coef.shape
    wide = rows + TILE
    shape = (wide, lanes)
    lane = lane_ids(shape)
    quad = lane // HALO
    part = lax.rem(quad, WIDE // HALO)
    if lax.axis_size("gy") == 2:
        from_right, from_left = from_one[...], from_two[...]
    else:
        even = is_even("gy")
        from_right = jnp.where(even, from_one[...], from_two[...])
        from_left = jnp.where(even, from_two[...], from_one[...])
    from_left = turn(from_left, 2 * HALO, 1)
    is_halo = jnp.logical_or(part == 3, part == 4)
    mixed = (
        jnp.where(lax.rem(quad, 2) == 0, from_right, from_left),
        jnp.where(lax.rem(quad, 2) == 0, from_left, from_right),
    )
    strip = []
    for c in range(8):
        value = jnp.where(is_halo, turn(mixed[c % 2], 3 * HALO - HALO * c, 1), own[c])
        strips[c] = value
        strip.append(value)
    last, first = pl.ds(rows - TILE, TILE), pl.ds(0, TILE)
    around = lambda low, tile, high: jnp.concatenate([low, tile, high], axis=0)
    main = {}
    for z in range(depth):
        for c in range(6):
            scale = slab_scale(c)
            main[c, z] = around(fields[c, z, last, :] * scale, halo[depth * c + z], fields[c, z, first, :] * scale)
    cells = [around(coef[z, last, :], halo[6 * depth + z], coef[z, first, :]) for z in range(depth)]
    cells.append(around(profile[last, :], halo[7 * depth], profile[first, :]))

    even = is_even("gz")
    bottom, top = lane < WIDE, lane >= WIDE * (depth - 1)
    upward = jnp.zeros(shape, F32)
    downward = jnp.zeros(shape, F32)

    for instant in range(HALO):
        ex, ey, ez = strip[0:3]
        z_ex = jnp.where(top, 0.0, turn(ex, -WIDE, 1))
        z_ey = jnp.where(top, 0.0, turn(ey, -WIDE, 1))
        y_ex, y_ez = turn(ex, -1, 1), turn(ez, -1, 1)
        rolled = alone_rolled(main, instant, depth, True)
        curl = curl_of_electric(ex, ey, ez, y_ex, y_ez, z_ex, z_ey)
        for c in range(2 if instant == HALO - 1 else 3):
            strip[3 + c] = strip[3 + c] - curl[c]
        alone_magnetic(main, instant, depth, rolled)
        for c in range(2):
            item = 2 * instant + c
            rows_at = wide + TILE * item
            ups = main[3 + c, depth - 1]
            downs = main[c, 0]
            for part_at, up_at, down_at in (
                (rows_at, TILE - instant - 1, TILE - instant),
                (rows_at + HALO, TILE + HALO + instant + 1, TILE + HALO + instant),
            ):
                up = ups[up_at : up_at + HALO, :]
                down = downs[down_at : down_at + HALO, :]
                to_a[part_at : part_at + HALO, :] = jnp.where(even, up, down)
                to_b[part_at : part_at + HALO, :] = jnp.where(even, down, up)
        electric = strip[0:3]
        if instant < HALO - 1:
            hx, hy, hz = strip[3:6]
            z_hx = jnp.where(bottom, 0.0, turn(hx, WIDE, 1))
            z_hy = jnp.where(bottom, 0.0, turn(hy, WIDE, 1))
            y_hx, y_hz = turn(hx, 1, 1), turn(hz, 1, 1)
            rolled = alone_rolled(main, instant, depth, False)
            back = curl_of_magnetic(hx, hy, hz, y_hx, y_hz, z_hx, z_hy)
            amount = plane_amount(table, instant, depth, depth)
            strip[0] = strip[0] + strip[6] * (back[0] + amount * strip[7])
            strip[1] = strip[1] + strip[6] * back[1]
            strip[2] = strip[2] + strip[6] * back[2]
            alone_electric(
                main,
                instant,
                depth,
                rolled,
                lambda p: cells[p],
                lambda p: plane_amount(table, instant, p, depth) * cells[depth],
            )
        for c in range(2):
            item = 2 * instant + c
            here = lane // GROUP == item
            both = jnp.where(lane < lanes // 2, electric[c], strip[3 + c])
            both = turn(both, GROUP * item - WIDE * (depth - 1) - TILE, 1)
            upward = jnp.where(here, both, upward)
            there = lane // GROUP == (item - WIDE * (depth - 1) // GROUP) % TRACES
            downward = jnp.where(there, both, downward)
    to_a[0:wide, :] = jnp.where(even, upward, downward)
    to_b[0:wide, :] = jnp.where(even, downward, upward)
    def send(at, up, down):
        if at < to_a.shape[0]:
            to_a[at : at + TILE, :] = jnp.where(even, up, down)
        if at < to_b.shape[0]:
            to_b[at : at + TILE, :] = jnp.where(even, down, up)

    at = wide + TILE * TRACES
    for beyond in range(BEYOND):
        send(at, halo[6 * depth + depth - 1 - beyond], halo[6 * depth + beyond])
        at += TILE
    side = lanes // (BEYOND * GROUP)
    tile_lane = lane_ids((TILE, lanes))
    for begin in range(0, wide // TILE, side):
        up = jnp.zeros((TILE, lanes), F32)
        down = jnp.zeros((TILE, lanes), F32)
        for tile in range(begin, min(begin + side, wide // TILE)):
            value = strips[6, TILE * tile : TILE * (tile + 1), :]
            for beyond in range(BEYOND):
                goal = GROUP * (BEYOND * (tile - begin) + beyond)
                here = tile_lane // GROUP == goal // GROUP
                z = depth - BEYOND + beyond
                up = jnp.where(here, turn(value, goal - WIDE * z - TILE, 1), up)
                down = jnp.where(here, turn(value, goal - WIDE * beyond - TILE, 1), down)
        send(at, up, down)
        at += TILE


def received(a, b, above, here):
    even = is_even("gz")
    one, two = (a, b) if above else (b, a)
    place = lax.axis_index("gz")
    exists = place < lax.axis_size("gz") - 1 if above else place > 0
    return jnp.where(exists, jnp.where(even, one[here], two[here]), 0.0)


def coef_beyond(a, b, above, p, depth, table, shape):
    size = lax.axis_size("gz")
    first, end = pillars(depth, size)
    z = lax.axis_index("gz") * depth + p - BEYOND
    base = HALO * (depth + 2)
    quarter = COURANT * COURANT
    low, high = quarter / table[base + 1 : base + 2, :], quarter / table[base : base + 1, :]
    layer = jnp.broadcast_to(jnp.where(z < first, low, high), shape)
    one = layer if a is None else a()
    two = layer if b is None else b()
    even = is_even("gz")
    value = jnp.where(even, one, two) if above else jnp.where(even, two, one)
    return jnp.where(jnp.logical_and(z >= 0, z < depth * size), value, 0.0)


def edges_after(ex_shifted, ez, lane):
    return jnp.where(lax.rem(lane, GROUP) == HALO - 1, ex_shifted, ez)


def edges_before(hx_shifted, hz, lane):
    return jnp.where(lax.rem(lane, GROUP) == 3 * HALO, hx_shifted, hz)


def arrived_kernel(*refs):
    pass


def rolled_after(main, mixed, planes, lane):
    end = lane.shape[1] - 1
    edge = {p: turn(mixed, -(GROUP * p + HALO), 1) for p in planes}
    ex = {p: turn(main[0, p], -1, 1) for p in planes}
    ez = {p: turn(jnp.where(lane == 0, edge[p], main[2, p]), -1, 1) for p in planes}
    return {p: (jnp.where(lane == end, edge[p], ex[p]), ez[p]) for p in planes}


def rolled_before(main, mixed, planes, lane):
    end = lane.shape[1] - 1
    edge = {p: turn(mixed, -(GROUP * p + 3 * HALO), 1) for p in planes}
    hx = {p: turn(main[3, p], 1, 1) for p in planes}
    hz = {p: turn(jnp.where(lane == end, edge[p], main[5, p]), 1, 1) for p in planes}
    return {p: (jnp.where(lane == 0, edge[p], hx[p]), hz[p]) for p in planes}


def below_factors(group):
    factor = jnp.where(lax.axis_index("gz") > 0, 1.0, 0.0)
    return factor, jnp.where(group < BEYOND, factor, 1.0)


def wide_field(fields, halo, c, z):
    depth = fields.shape[1]
    own = fields[c, z] * slab_scale(c) if c >= 3 else fields[c, z]
    return jnp.concatenate([own, halo[depth * c + z]], axis=0)


def prepare_kernel(
    fields, halo, coef, profile, table, wide_strips, early, strips, magnetic, shifted, electric, shifted_on, inner, shifted_inner, out
):
    _, wide, lanes = wide_strips.shape
    depth = lanes // WIDE
    first, last = BEYOND, BEYOND + depth - 1
    lane = lane_ids((TILE, lanes))
    for at in range(0, wide, TILE):
        here = pl.ds(at, TILE)
        for c in range(8):
            value = wide_strips[c, here, :]
            moved = jnp.zeros((TILE, lanes), F32)
            for z in range(depth):
                goal = GROUP * (z + BEYOND)
                moved = jnp.where(lane // GROUP == z + BEYOND, turn(value, goal - WIDE * z - TILE, 1), moved)
            strips[c, here, :] = moved
    lane = lane_ids((wide, lanes))
    below_factor, strip_factor = below_factors(lane // GROUP)
    ex, ey, ez, hx, hy, hz = [strips[c] for c in range(6)]
    y_ex, y_ez = turn(ex, -1, 1), turn(ez, -1, 1)
    curl = curl_of_electric(ex, ey, ez, y_ex, y_ez, turn(ex, -GROUP, 1), turn(ey, -GROUP, 1))
    hx, hy, hz = [value - strip_factor * curl[c] for c, value in enumerate((hx, hy, hz))]
    for c, value in enumerate((hx, hy, hz)):
        magnetic[c, depth + 1] = value
    zero = jnp.zeros((wide, lanes), F32)
    main = {(c, first + z): wide_field(fields, halo, c, z) for c in range(6) for z in range(depth)}
    for c in range(6):
        main[c, first - 1] = main[c, last + 1] = zero
    moved = rolled_after(main, edges_after(y_ex, ez, lane), range(first, last + 1), lane)
    mixed = edges_before(turn(hx, 1, 1), hz, lane)
    for p in range(first - 1, last + 1):
        curl = curl_of_electric(
            main[0, p], main[1, p], main[2, p], *moved.get(p, (zero, zero)), main[0, p + 1], main[1, p + 1]
        )
        for c in range(3):
            main[3 + c, p] = main[3 + c, p] - (curl[c] if p >= first else below_factor * curl[c])
            magnetic[c, p - first + 1] = main[3 + c, p]
    moved = rolled_before(main, mixed, range(first - 1, last), lane)
    for p in range(first - 1, last):
        shifted[0, p - first + 1], shifted[1, p - first + 1] = moved[p]
    back = curl_of_magnetic(hx, hy, hz, turn(hx, 1, 1), turn(hz, 1, 1), turn(hx, GROUP, 1), turn(hy, GROUP, 1))
    ex = ex + strips[6] * (back[0] + plane_amount(table, 0, depth + 1, depth) * strips[7])
    ey = ey + strips[6] * back[1]
    ez = ez + strips[6] * back[2]
    y_ex, y_ez = turn(ex, -1, 1), turn(ez, -1, 1)
    wide_profile = jnp.concatenate([profile[...], halo[7 * depth]], axis=0)
    for p in range(first, last):
        z = p - first
        back = curl_of_magnetic(main[3, p], main[4, p], main[5, p], *moved[p], main[3, p - 1], main[4, p - 1])
        back = (back[0] + plane_amount(table, 0, z, depth) * wide_profile, back[1], back[2])
        here = jnp.concatenate([coef[z], halo[6 * depth + z]], axis=0)
        for c in range(3):
            main[c, p] = main[c, p] + here * back[c]
            electric[c, z] = main[c, p]
    between = range(first + 1, last)
    moved = rolled_after(main, edges_after(y_ex, ez, lane), between, lane)
    for p in between:
        shifted_on[0, p - first - 1], shifted_on[1, p - first - 1] = moved[p]
    curl = curl_of_electric(ex, ey, ez, y_ex, y_ez, turn(ex, -GROUP, 1), turn(ey, -GROUP, 1))
    hx, hz = hx - strip_factor * curl[0], hz - strip_factor * curl[2]
    for p in range(first + 1, last - 1):
        curl = curl_of_electric(
            main[0, p], main[1, p], main[2, p], *moved[p], main[0, p + 1], main[1, p + 1]
        )
        for c in range(3):
            main[3 + c, p] = main[3 + c, p] - curl[c]
            inner[c, p - first - 1] = main[3 + c, p]
    mixed = edges_before(turn(hx, 1, 1), hz, lane)
    moved = rolled_before(main, mixed, range(first + 1, last - 1), lane)
    for p in range(first + 1, last - 1):
        shifted_inner[0, p - first - 1], shifted_inner[1, p - first - 1] = moved[p]


def window_kernel(
    fields,
    coef,
    profile,
    halo,
    table,
    strips,
    magnetic,
    shifted,
    electric,
    shifted_on,
    inner,
    shifted_inner,
    early_a,
    early_b,
    late_a,
    late_b,
    forward,
    material,
    fields_out,
    eps_grad,
    results,
    grad,
    sems,
    *beside,
):
    depth, rows, lanes = material.shape
    wide = rows + TILE
    shape = (wide, lanes)
    own = range(BEYOND, BEYOND + depth)
    first, last = own[0], own[-1]
    lane = lane_ids(shape)
    group = lane // GROUP

    late_strips = [received(late_a, late_b, above, slice(0, wide)) for above in (False, True)]
    late_strips[True] = turn(late_strips[True], WIDE * (depth - 1), 1)
    places, early_end = early_rows(rows)
    traces = {}

    def merge(above, item):
        lost = item // 2 if above else item // 2 + 1
        whole = beside[TRACES * above + item]
        at, low, high = places[item]
        whole[low:high, :] = received(early_a, early_b, above, slice(at, at + high - low))
        at = wide + TILE * item
        right = received(late_a, late_b, above, slice(at, at + HALO))
        left = received(late_a, late_b, above, slice(at + HALO, at + TILE))
        whole[rows - lost : rows - lost + HALO, :] = right
        if lost < HALO:
            whole[rows + HALO + lost : wide, :] = left[0 : HALO - lost]
        if lost > 0:
            whole[0:lost, :] = left[HALO - lost : HALO]
        value = whole[...]
        if lost > 0:
            edge = turn(late_strips[above], lanes - HALO - GROUP * item, 1)
            value = jnp.where(lane >= lanes - lost, edge, value)
        lost_left = lost if above else lost - 1
        if lost_left > 0:
            edge = turn(late_strips[above], -(GROUP * item + 3 * HALO), 1)
            value = jnp.where(lane < lost_left, edge, value)
        traces[above, item] = value

    def trace(above, item):
        return traces[above, item]

    def strip_neighbours(above, item, one, two):
        goal = last if above else first - 1
        moved = turn(late_strips[above], GROUP * (goal - item), 1)
        at_goal, at_next = group == goal, group == goal + 1
        by = -GROUP if above else GROUP
        if above:
            one = turn(one, by, 1)
            two = turn(jnp.where(at_next, two + moved, two), by, 1)
            return jnp.where(at_goal, one + moved, one), two
        one = turn(jnp.where(at_goal, one + moved, one), by, 1)
        two = turn(two, by, 1)
        return one, jnp.where(at_next, two + moved, two)

    at = wide + TILE * TRACES
    lates = [late if late.shape[0] > at else None for late in (late_a, late_b)]
    joined = lambda top, tile: jnp.concatenate([top, tile], axis=0)
    zero = jnp.zeros(shape, F32)

    def late_tile(here, shift=0):
        return [None if late is None else (lambda late=late: turn(late[here], shift, 1)) for late in lates]

    wide_coef = {first + z: joined(coef[z], halo[6 * depth + z]) for z in range(depth)}
    for beyond in range(BEYOND):
        for above in (False, True):
            p = last + 1 + beyond if above else first - 1 - beyond
            from_early = slice(early_end + rows * beyond, early_end + rows * (beyond + 1))
            parts = [
                None if early.shape[0] == early_end else (lambda early=early: early[from_early])
                for early in (early_a, early_b)
            ]
            top = coef_beyond(*parts, above, p, depth, table, (rows, lanes))
            parts = late_tile(slice(at, at + TILE))
            wide_coef[p] = joined(top, coef_beyond(*parts, above, p, depth, table, (TILE, lanes)))
        at += TILE
    side = lanes // (BEYOND * GROUP)
    tile_group = lane_ids((TILE, lanes)) // GROUP
    tiles = []
    for tile in range(wide // TILE):
        here = slice(at + TILE * (tile // side), at + TILE * (tile // side) + TILE)
        start = BEYOND * GROUP * (tile % side)
        value = strips[6, TILE * tile : TILE * (tile + 1), :]
        low = coef_beyond(*late_tile(here, -start), False, tile_group, depth, table, (TILE, lanes))
        parts = late_tile(here, GROUP * (last + 1) - start)
        high = coef_beyond(*parts, True, tile_group, depth, table, (TILE, lanes))
        value = jnp.where(tile_group < first, low, value)
        tiles.append(jnp.where(tile_group > last, high, value))
    strip_coef = jnp.concatenate(tiles, axis=0)
    wide_profile = joined(profile[...], halo[7 * depth])
    strip = [strips[c] for c in range(6)]
    main = {(c, p): zero for c in range(6) for p in range(first - BEYOND, last + BEYOND + 1)}
    for c in range(3):
        for z in range(depth):
            main[c, first + z] = wide_field(fields, halo, c, z)
        for p in range(first - 1, last + 1):
            main[3 + c, p] = magnetic[c, p - first + 1]
        strip[3 + c] = magnetic[c, depth + 1]
    below_factor, strip_factor = below_factors(group)

    copies = []

    def hand_out(source, target):
        copy = pltpu.make_async_copy(source, target, sems.at[len(copies)])
        copy.start()
        copies.append(copy)

    def magnetic_planes(instant):
        above = min(instant, HALO - 1 - instant, BEYOND - 1)
        return list(range(first - min(instant + 1, HALO - instant, BEYOND), last + above + 1))

    def electric_planes(instant):
        reach = min(instant + 1, HALO - 1 - instant, BEYOND)
        return list(range(first - reach, last + reach + 1))

    def in_groups(planes):
        size = -(-len(planes) // GROUPS)
        return [planes[at : at + size] for at in range(0, len(planes), size)]

    def strip_magnetic(instant):
        ex, ey, ez = strip[0:3]
        curl = curl_of_electric(ex, ey, ez, *strip_shifts)
        for c in range(3):
            strip[3 + c] = strip[3 + c] - strip_factor * curl[c]
        return strip_shifted_magnetic(instant)

    def strip_shifted_magnetic(instant):
        hx, hy, hz = strip[3:6]
        y_hx, y_hz = turn(hx, 1, 1), turn(hz, 1, 1)
        z_hx, z_hy = strip_neighbours(False, 2 * instant, hx, hy)
        return (y_hx, y_hz, z_hx, z_hy), edges_before(y_hx, hz, lane)

    def strip_shifted_electric(instant):
        ex, ey, ez = strip[0:3]
        y_ex, y_ez = turn(ex, -1, 1), turn(ez, -1, 1)
        z_ex, z_ey = strip_neighbours(True, 2 * instant, ex, ey)
        return (y_ex, y_ez, z_ex, z_ey), edges_after(y_ex, ez, lane)

    def strip_electric(instant):
        back = curl_of_magnetic(*strip[3:6], *strip_shifts)
        amount = plane_amount(table, instant, depth + 1, depth)
        strip[0] = strip[0] + strip_coef * (back[0] + amount * strips[7])
        strip[1] = strip[1] + strip_coef * back[1]
        strip[2] = strip[2] + strip_coef * back[2]
        return strip_shifted_electric(instant + 1)

    total = [None] * depth
    merge(True, 0)
    merge(True, 1)
    at_last = group == last
    strip[3] = jnp.where(at_last, strip[3] + turn(late_strips[True], GROUP * (last - 1), 1), strip[3])
    strip[4] = jnp.where(at_last, strip[4] - turn(late_strips[True], GROUP * last, 1), strip[4])
    main[3, last] = main[3, last] + trace(True, 1)
    main[4, last] = main[4, last] - trace(True, 0)
    strip_shifts, mixed = strip_shifted_magnetic(0)
    moved = {p: (shifted[0, p - first + 1], shifted[1, p - first + 1]) for p in range(first - 1, last)}
    moved[last + 1] = (zero, zero)
    for instant in range(HALO):
        item = 2 * instant
        final = instant == HALO - 1

        mixed_now = mixed
        if not final:
            strip_shifts, mixed = strip_electric(instant)
        merge(False, item)
        merge(False, item + 1)
        ready = range(first + 1, last - 1) if instant == 1 else ()
        if instant == 0:
            moved.update(rolled_before(main, mixed_now, [last], lane))
        else:
            following = electric_planes(instant)
            later = {p: (zero, zero) for p in following}
            for planes in in_groups(magnetic_planes(instant)):
                for p in planes:
                    if p in ready:
                        for c in range(3):
                            main[3 + c, p] = inner[c, p - first - 1]
                        later[p] = (shifted_inner[0, p - first - 1], shifted_inner[1, p - first - 1])
                        continue
                    z_ex, z_ey = main[0, p + 1], main[1, p + 1]
                    if p == last:
                        z_ex, z_ey = z_ex + trace(True, item), z_ey + trace(True, item + 1)
                    curl = curl_of_electric(
                        main[0, p], main[1, p], main[2, p], *moved.get(p, (zero, zero)), z_ex, z_ey
                    )
                    for c in range(3):
                        main[3 + c, p] = main[3 + c, p] - (curl[c] if p >= first else below_factor * curl[c])
                        if final and first <= p <= last:
                            results[3 + c, p - first] = main[3 + c, p][0:rows] * COURANT
                    if final and first <= p <= last:
                        z = p - first
                        hand_out(results.at[pl.ds(3, 3), z], fields_out.at[pl.ds(3, 3), z])
                later.update(rolled_before(main, mixed_now, [p for p in planes if p in following and p not in ready], lane))
            moved = later

        mixed_now = mixed
        if not final:
            strip_shifts, mixed = strip_magnetic(instant + 1)
            merge(True, item + 2)
            merge(True, item + 3)
        following = [] if final else magnetic_planes(instant + 1)
        later = {}
        for planes in in_groups(electric_planes(instant)):
            for p in planes:
                z_hx, z_hy = main.get((3, p - 1), zero), main.get((4, p - 1), zero)
                if p == first:
                    z_hx, z_hy = z_hx + trace(False, item), z_hy + trace(False, item + 1)
                here = wide_coef[p]
                inside = first <= p <= last
                z = p - first
                there = instant == 0 and first <= p < last
                back = None
                if not there:
                    back = curl_of_magnetic(main[3, p], main[4, p], main[5, p], *moved[p], z_hx, z_hy)
                if inside and not there:
                    push = plane_amount(table, instant, z, depth) * wide_profile
                    back = (back[0] + push, back[1], back[2])
                for c in range(3):
                    main[c, p] = electric[c, z] if there else main[c, p] + here * back[c]
                    if there and p == first and c < 2:
                        enters = here * trace(False, item + 1 - c)
                        main[c, p] = main[c, p] + enters if c == 0 else main[c, p] - enters
                    if inside:
                        term = forward[instant, c, z].astype(F32) * main[c, p][0:rows]
                        total[z] = term if total[z] is None else total[z] + term
                if inside and final:
                    for c in range(3):
                        results[c, z] = main[c, p][0:rows]
                    grad[z] = jnp.where(material[z] >= 2, -total[z], 0.0)
                    hand_out(results.at[pl.ds(0, 3), z], fields_out.at[pl.ds(0, 3), z])
                    hand_out(grad.at[z], eps_grad.at[z])
            given = [p for p in planes if instant == 0 and first < p < last]
            later.update(
                rolled_after(main, mixed_now, [p for p in planes if p in following and p not in given], lane)
            )
            later.update({p: (shifted_on[0, p - first - 1], shifted_on[1, p - first - 1]) for p in given})
        moved = later
    for copy in copies:
        copy.wait()


VMEM = pl.BlockSpec(memory_space=pltpu.VMEM)
FAR = pl.BlockSpec(memory_space=pltpu.HBM)


def near(array):
    return pltpu.with_memory_space_constraint(array, pltpu.VMEM)


def far_off(array):
    return pltpu.with_memory_space_constraint(array, pltpu.HBM), FAR


def call(kernel, operands, outs, scratch=(), far=0, aliases=None, name=None, cost=None):
    specs, arrays = [], []
    for operand in operands:
        if isinstance(operand, tuple):
            specs.append(operand[1])
            arrays.append(operand[0])
        else:
            specs.append(VMEM)
            arrays.append(near(operand))
    return pl.pallas_call(
        kernel,
        out_shape=[jax.ShapeDtypeStruct(s, F32) for s in outs[:far]] + [
            pltpu.VMEM(getattr(s, "shape", s), getattr(s, "dtype", F32)) for s in outs[far:]
        ],
        in_specs=specs,
        out_specs=[FAR] * far + [VMEM] * (len(outs) - far),
        scratch_shapes=[s if not isinstance(s, tuple) else pltpu.VMEM(s, F32) for s in scratch],
        input_output_aliases=aliases or {},
        compiler_params=pltpu.CompilerParams(vmem_limit_bytes=32 * 1024 * 1024),
        cost_estimate=cost,
        name=name,
    )(*arrays)


def on_device(
    fields_in, material, material_eps, source_plane, source_wave, source_profile, forward_fields
):
    depth, rows, lanes = material.shape
    assert source_wave.shape[0] == HALO and depth * WIDE == lanes and BEYOND <= depth
    assert (depth + 2 * BEYOND) * GROUP == lanes and TRACES * GROUP == lanes
    wide = rows + TILE
    slabs = 7 * depth + 1
    tiles = (slabs + 1) // 2

    inputs = (fields_in, material, source_profile, material_eps, source_wave)
    to_a, to_b, scalars, material, source_profile = call(
        x_pack_kernel,
        [far_off(array) for array in inputs],
        [(tiles, TILE, lanes)] * 2
        + [(HALO + material_eps.shape[0], lanes), material, source_profile.shape],
        [
            (2, 6, depth, TILE, lanes),
            pltpu.SMEM(material_eps.shape, F32),
            pltpu.SMEM(source_wave.shape, F32),
            pltpu.SemaphoreType.DMA((6,)),
        ],
        name="x_pack",
    )
    swap_a, swap_b = swaps(lax.axis_size("gx"), True)
    from_a = lax.ppermute(to_a, "gx", swap_a)
    from_b = lax.ppermute(to_b, "gx", swap_b)

    pairs_a, z_a, pairs_b, z_b = z_swaps(lax.axis_size("gz"), lax.axis_size("gx"))
    with_coef = [sends_coef(depth, lax.axis_size("gz"), pairs) for pairs in (pairs_a, pairs_b)]
    early_counts = [early_rows(rows)[1] + rows * BEYOND * sent for sent in with_coef]
    plane = jnp.broadcast_to(source_plane[None], (1, lanes))
    coef, early_a, early_b, partly, table = call(
        interior_kernel,
        [fields_in, material, source_profile, scalars, plane],
        [(depth, rows, lanes)]
        + [(count, lanes) for count in early_counts]
        + [(2, wide, lanes), (HALO * (depth + 2) + material_eps.shape[0], lanes)],
        name="interior",
    )
    halo, y_out = call(
        x_unpack_kernel,
        [from_a, from_b, partly],
        [(slabs, TILE, lanes), (2, wide, lanes)],
        aliases={2: 1},
        name="x_unpack",
    )
    swap_a, swap_b = swaps(lax.axis_size("gy"), True)
    if lax.axis_size("gy") == 2:
        both = lax.ppermute(y_out, "gy", swap_a)
        from_one, from_two = both[0], both[1]
    else:
        from_one = lax.ppermute(y_out[0], "gy", swap_a)
        from_two = lax.ppermute(y_out[1], "gy", swap_b)

    early_a = lax.ppermute(early_a, ("gz", "gx"), z_a)
    early_b = lax.ppermute(early_b, ("gz", "gx"), z_b)
    (own,) = call(
        own_strips_kernel,
        [fields_in, coef, source_profile, halo],
        [(8, wide, lanes)],
        name="own_strips",
    )
    side = lanes // (BEYOND * GROUP)
    coef_rows = TILE * BEYOND + TILE * (-(-wide // TILE // side))
    late_rows = [wide + TILE * TRACES + coef_rows * sent for sent in with_coef]
    strips, late_a, late_b = call(
        frame_kernel,
        [fields_in, coef, source_profile, table, halo, own, from_one, from_two],
        [(8, wide, lanes)] + [(count, lanes) for count in late_rows],
        name="frame",
    )
    late_a = lax.ppermute(late_a, ("gz", "gx"), z_a)
    late_b = lax.ppermute(late_b, ("gz", "gx"), z_b)

    (early_b,) = call(
        arrived_kernel,
        [early_b],
        [early_b.shape],
        aliases={0: 0},
        name="arrived",
        cost=pl.CostEstimate(flops=10**9, bytes_accessed=0, transcendentals=0),
    )
    strips, *prepared, early_b = call(
        prepare_kernel,
        [fields_in, halo, coef, source_profile, table, strips, early_b],
        [(8, wide, lanes), (3, depth + 2, wide, lanes), (2, depth, wide, lanes), (3, depth - 1, wide, lanes)]
        + [(2, depth - 2, wide, lanes), (3, depth - 3, wide, lanes), (2, depth - 3, wide, lanes), early_b.shape],
        aliases={6: 7},
        name="prepare",
    )
    fields_out, eps_grad = call(
        window_kernel,
        [fields_in, coef, source_profile, halo, table, strips, *prepared]
        + [early_a, early_b, late_a, late_b]
        + [forward_fields, material],
        [(6, depth, rows, lanes), (depth, rows, lanes)],
        [
            (6, depth, rows, lanes),
            (depth, rows, lanes),
            pltpu.SemaphoreType.DMA((3 * depth,)),
        ]
        + [(wide, lanes)] * (2 * TRACES),
        far=2,
        name="window",
    )
    return (fields_out, eps_grad)


def solution(mesh):
    placed = (
        P(None, "gz", "gx", "gy"),
        P("gz", "gx", "gy"),
        P(),
        P(),
        P(),
        P("gx", "gy"),
        P(None, None, "gz", "gx", "gy"),
    )
    return jax.shard_map(
        on_device,
        mesh=mesh,
        in_specs=placed,
        out_specs=(P(None, "gz", "gx", "gy"), P("gz", "gx", "gy")),
        check_vma=False,
    )
```

```python
import jax
import jax.numpy as jnp
from jax import lax
from jax.experimental import pallas as pl
from jax.experimental.pallas import tpu as pltpu
from jax.sharding import PartitionSpec as P

COURANT = 0.5
HALO = 4
BEYOND = 2
TILE = 8
GROUP = 16
WIDE = 32
TRACES = 2 * HALO
GROUPS = 1
F32 = jnp.float32


def lane_ids(shape):
    return lax.broadcasted_iota(jnp.int32, shape, 1)


def row_ids(shape):
    return lax.broadcasted_iota(jnp.int32, shape, 0)


def turn(value, shift, axis):
    shift = shift % value.shape[axis]
    if shift == 0:
        return value
    return pltpu.roll(value, shift, axis)


def x_after(value):
    return turn(value, -1, 0)


def x_before(value):
    return turn(value, 1, 0)


def early_rows(rows):
    places, at = [], 0
    for item in range(TRACES):
        cut = item // 2
        places.append((at, cut, rows - cut))
        at += rows - 2 * cut
    return places, at


def swaps(size, periodic):
    first = [(i, i + 1) for i in range(0, size - 1, 2)]
    second = [(i, i + 1) for i in range(1, size - 1, 2)]
    if periodic and size > 2:
        second.append((size - 1, 0))
    both = lambda pairs: pairs + [(b, a) for a, b in pairs]
    return both(first), both(second)


def z_swaps(size, beside):
    first, second = swaps(size, False)
    wide = lambda pairs: [(a * beside + i, b * beside + i) for a, b in pairs for i in range(beside)]
    idle = [z for z in range(size) if all(z != a for a, _ in second)]
    cores = [(z * beside + i, z * beside + (i ^ 1)) for z in idle for i in range(beside)]
    return first, wide(first), second, wide(second) + cores


def pillars(depth, size):
    planes = depth * size
    return planes * 3 // 8, planes * 5 // 8


def sends_coef(depth, size, pairs):
    first, end = pillars(depth, size)
    edges = [max(a, b) * depth for a, b in pairs]
    return any(edge - BEYOND < end and edge + BEYOND > first for edge in edges)


def is_even(axis):
    return lax.rem(lax.axis_index(axis), 2) == 0


def coef_of(which, eps, count):
    permit = jnp.zeros(which.shape, F32)
    for index in range(count):
        permit = jnp.where(which == index, eps(index), permit)
    return (COURANT * COURANT) / permit


def slab_scale(c):
    return 1.0 / COURANT if 3 <= c < 6 else 1.0


def x_pack_kernel(
    fields, material, profile, eps, wave, to_a, to_b, scalars, material_in, profile_in, face, eps_in, wave_in, sems
):
    depth, rows, lanes = material.shape
    pairs = [(material, material_in), (profile, profile_in), (eps, eps_in), (wave, wave_in)]
    pairs = [(fields.at[:, :, pl.ds(at, TILE), :], face.at[i]) for i, at in enumerate((0, rows - TILE))] + pairs
    copies = [pltpu.make_async_copy(one, two, sems.at[index]) for index, (one, two) in enumerate(pairs)]
    for copy in copies:
        copy.start()
    for copy in copies:
        copy.wait()
    even = is_even("gx")
    upper = row_ids((TILE, lanes)) < HALO

    def slab(side, s):
        c, z = divmod(s, depth)
        here = slice(0, TILE) if side == 0 else slice(rows - TILE, rows)
        if c < 6:
            return face[side, c, z] * slab_scale(c)
        if c == 6:
            return coef_of(material_in[z, here, :], lambda index: eps_in[index], eps.shape[0])
        return profile_in[here, :]

    count = 7 * depth + 1
    for tile in range(to_a.shape[0]):
        one, two = 2 * tile, min(2 * tile + 1, count - 1)
        left = jnp.where(upper, slab(0, one), turn(slab(0, two), HALO, 0))
        right = jnp.where(upper, turn(slab(1, one), HALO, 0), slab(1, two))
        to_a[tile] = jnp.where(even, right, left)
        to_b[tile] = jnp.where(even, left, right)
    values = [wave_in[t] * (1.0 / COURANT) for t in range(HALO)] + [eps_in[i] for i in range(eps.shape[0])]
    for index, value in enumerate(values):
        scalars[index : index + 1, :] = jnp.full((1, lanes), value)


def y_pack_tile(slab, depth, lanes):
    quad = lane_ids((TILE, lanes)) // HALO
    low = jnp.zeros((TILE, lanes), F32)
    high = jnp.zeros((TILE, lanes), F32)
    for c in range(8):
        for z in range(depth):
            value = slab(c, z)
            at = WIDE * z + HALO * c
            moved = turn(value, at, 1)
            low = jnp.where(quad == at // HALO, moved, low)
            high = jnp.where(quad == (at // HALO - 1) % (lanes // HALO), moved, high)
    return low, high


def y_place(out, at, low, high, both):
    here = pl.ds(at, TILE)
    if both:
        out[0, here, :], out[1, here, :] = low, high
    else:
        even = is_even("gy")
        out[0, here, :] = jnp.where(even, high, low)
        out[1, here, :] = jnp.where(even, low, high)


def x_unpack_kernel(from_b, from_a, partly, halo, out):
    depth = (halo.shape[0] - 1) // 7
    lanes = halo.shape[2]
    even = is_even("gx")
    upper = row_ids((TILE, lanes)) < HALO
    count = halo.shape[0]
    for tile in range(from_a.shape[0]):
        a, b = from_a[tile], from_b[tile]
        right = jnp.where(even, a, b)
        left = jnp.where(even, b, a)
        halo[2 * tile] = jnp.where(upper, right, turn(left, HALO, 0))
        if 2 * tile + 1 < count:
            halo[2 * tile + 1] = jnp.where(upper, turn(right, HALO, 0), left)
    slab = lambda c, z: halo[depth * c + z] if c < 7 else halo[7 * depth]
    low, high = y_pack_tile(slab, depth, lanes)
    y_place(out, out.shape[1] - TILE, low, high, lax.axis_size("gy") == 2)


def plane_amount(table, instant, z, depth):
    at = instant * (depth + 2) + z
    return table[at : at + 1, :]


def curl_of_electric(ex, ey, ez, y_ex, y_ez, z_ex, z_ey):
    curl_x = (y_ez - ez) - (z_ey - ey)
    curl_y = (z_ex - ex) - (x_after(ez) - ez)
    curl_z = (x_after(ey) - ey) - (y_ex - ex)
    return curl_x, curl_y, curl_z


def curl_of_magnetic(hx, hy, hz, y_hx, y_hz, z_hx, z_hy):
    back_x = (hz - y_hz) - (hy - z_hy)
    back_y = (hx - z_hx) - (hz - x_before(hz))
    back_z = (hy - x_before(hy)) - (hx - y_hx)
    return back_x, back_y, back_z


def alone_planes(depth, instant):
    every = list(range(depth))
    left = HALO - 1 - instant
    if left == 0:
        return [depth - 1], []
    if left == 1:
        return sorted({0, depth - 2, depth - 1} & set(every)), sorted({0, depth - 1})
    return every, every


def alone_rolled(main, instant, depth, magnetic):
    planes = alone_planes(depth, instant)[0 if magnetic else 1]
    one, two, by = (0, 2, -1) if magnetic else (3, 5, 1)
    return {p: (turn(main[one, p], by, 1), turn(main[two, p], by, 1)) for p in planes}


def alone_magnetic(main, instant, depth, rolled):
    for p in alone_planes(depth, instant)[0]:
        ex, ey, ez = main[0, p], main[1, p], main[2, p]
        zero = jnp.zeros_like(ex)
        z_ex, z_ey = (main[0, p + 1], main[1, p + 1]) if p + 1 < depth else (zero, zero)
        curl = curl_of_electric(ex, ey, ez, *rolled[p], z_ex, z_ey)
        for c in range(2 if instant == HALO - 1 else 3):
            main[3 + c, p] = main[3 + c, p] - curl[c]


def alone_electric(main, instant, depth, rolled, coef, source):
    for p in alone_planes(depth, instant)[1]:
        hx, hy, hz = main[3, p], main[4, p], main[5, p]
        zero = jnp.zeros_like(hx)
        z_hx, z_hy = (main[3, p - 1], main[4, p - 1]) if p > 0 else (zero, zero)
        back = curl_of_magnetic(hx, hy, hz, *rolled[p], z_hx, z_hy)
        here = coef(p)
        main[0, p] = main[0, p] + here * (back[0] + source(p))
        main[1, p] = main[1, p] + here * back[1]
        main[2, p] = main[2, p] + here * back[2]


def interior_kernel(
    fields, material, profile, scalars, plane, coef, to_a, to_b, y_out, table
):
    depth, rows, lanes = material.shape
    eps = lambda index: scalars[HALO + index : HALO + index + 1, :]
    lane = lane_ids((1, lanes))
    there = plane[...] - lax.axis_index("gz") * depth
    inside = jnp.logical_and(there >= 0, there < depth)
    groups = [jnp.full((1, lanes), z, jnp.int32) for z in range(depth)]
    groups += [lane // WIDE, lane // GROUP - BEYOND]
    for instant in range(HALO):
        amount = jnp.where(inside, scalars[instant : instant + 1, :], 0.0)
        for index, group in enumerate(groups):
            at = instant * len(groups) + index
            table[at : at + 1, :] = jnp.where(group == there, amount, 0.0)
    base = HALO * len(groups)
    count = scalars.shape[0] - HALO
    table[base : base + count, :] = scalars[HALO : HALO + count, :]
    for z in range(depth):
        coef[z] = coef_of(material[z], eps, count)

    even = is_even("gz")

    places, end = early_rows(rows)

    def send(at, upward, downward):
        here = slice(at, at + upward.shape[0])
        if at < to_a.shape[0]:
            to_a[here, :] = jnp.where(even, upward, downward)
        if at < to_b.shape[0]:
            to_b[here, :] = jnp.where(even, downward, upward)

    for beyond in range(BEYOND):
        send(end + rows * beyond, coef[depth - 1 - beyond], coef[beyond])
    for at in range(0, rows, TILE):
        here = pl.ds(at, TILE)

        def slab(c, z):
            if c < 6:
                return fields[c, z, here, :] * slab_scale(c)
            return coef[z, here, :] if c == 6 else profile[here, :]

        low, high = y_pack_tile(slab, depth, lanes)
        y_place(y_out, at, low, high, lax.axis_size("gy") == 2)
    main = {(c, z): fields[c, z] * slab_scale(c) for c in range(6) for z in range(depth)}
    for instant in range(HALO):
        alone_magnetic(main, instant, depth, alone_rolled(main, instant, depth, True))
        for c in range(2):
            at, low, high = places[2 * instant + c]
            send(at, main[3 + c, depth - 1][low:high], main[c, 0][low:high])
        if instant < HALO - 1:
            alone_electric(
                main,
                instant,
                depth,
                alone_rolled(main, instant, depth, False),
                lambda p: coef[p],
                lambda p: plane_amount(table, instant, p, depth) * profile[...],
            )


def own_strips_kernel(fields, coef, profile, halo, strips):
    depth, rows, lanes = coef.shape
    for at in range(0, rows + TILE, TILE):
        here = pl.ds(at, TILE)
        lane = lane_ids((TILE, lanes))
        part = lax.rem(lane, WIDE) // HALO
        on_right = jnp.logical_or(part == 1, part == 2)
        for c in range(8):
            out = jnp.zeros((TILE, lanes), F32)
            for z in range(depth):
                if at == rows:
                    value = halo[depth * c + z] if c < 7 else halo[7 * depth]
                elif c < 6:
                    value = fields[c, z, here, :] * slab_scale(c)
                else:
                    value = coef[z, here, :] if c == 6 else profile[here, :]
                first = WIDE * z + HALO
                both = jnp.where(on_right, turn(value, first + 2 * HALO, 1), turn(value, first + 4 * HALO, 1))
                out = jnp.where(lane // WIDE == z, both, out)
            strips[c, here, :] = out


def frame_kernel(
    fields, coef, profile, table, halo, own, from_one, from_two, strips, to_a, to_b
):
    depth, rows, lanes = coef.shape
    wide = rows + TILE
    shape = (wide, lanes)
    lane = lane_ids(shape)
    quad = lane // HALO
    part = lax.rem(quad, WIDE // HALO)
    if lax.axis_size("gy") == 2:
        from_right, from_left = from_one[...], from_two[...]
    else:
        even = is_even("gy")
        from_right = jnp.where(even, from_one[...], from_two[...])
        from_left = jnp.where(even, from_two[...], from_one[...])
    from_left = turn(from_left, 2 * HALO, 1)
    is_halo = jnp.logical_or(part == 3, part == 4)
    mixed = (
        jnp.where(lax.rem(quad, 2) == 0, from_right, from_left),
        jnp.where(lax.rem(quad, 2) == 0, from_left, from_right),
    )
    strip = []
    for c in range(8):
        value = jnp.where(is_halo, turn(mixed[c % 2], 3 * HALO - HALO * c, 1), own[c])
        strips[c] = value
        strip.append(value)
    last, first = pl.ds(rows - TILE, TILE), pl.ds(0, TILE)
    around = lambda low, tile, high: jnp.concatenate([low, tile, high], axis=0)
    main = {}
    for z in range(depth):
        for c in range(6):
            scale = slab_scale(c)
            main[c, z] = around(fields[c, z, last, :] * scale, halo[depth * c + z], fields[c, z, first, :] * scale)
    cells = [around(coef[z, last, :], halo[6 * depth + z], coef[z, first, :]) for z in range(depth)]
    cells.append(around(profile[last, :], halo[7 * depth], profile[first, :]))

    even = is_even("gz")
    bottom, top = lane < WIDE, lane >= WIDE * (depth - 1)
    upward = jnp.zeros(shape, F32)
    downward = jnp.zeros(shape, F32)

    for instant in range(HALO):
        ex, ey, ez = strip[0:3]
        z_ex = jnp.where(top, 0.0, turn(ex, -WIDE, 1))
        z_ey = jnp.where(top, 0.0, turn(ey, -WIDE, 1))
        y_ex, y_ez = turn(ex, -1, 1), turn(ez, -1, 1)
        rolled = alone_rolled(main, instant, depth, True)
        curl = curl_of_electric(ex, ey, ez, y_ex, y_ez, z_ex, z_ey)
        for c in range(2 if instant == HALO - 1 else 3):
            strip[3 + c] = strip[3 + c] - curl[c]
        alone_magnetic(main, instant, depth, rolled)
        for c in range(2):
            item = 2 * instant + c
            rows_at = wide + TILE * item
            ups = main[3 + c, depth - 1]
            downs = main[c, 0]
            for part_at, up_at, down_at in (
                (rows_at, TILE - instant - 1, TILE - instant),
                (rows_at + HALO, TILE + HALO + instant + 1, TILE + HALO + instant),
            ):
                up = ups[up_at : up_at + HALO, :]
                down = downs[down_at : down_at + HALO, :]
                to_a[part_at : part_at + HALO, :] = jnp.where(even, up, down)
                to_b[part_at : part_at + HALO, :] = jnp.where(even, down, up)
        electric = strip[0:3]
        if instant < HALO - 1:
            hx, hy, hz = strip[3:6]
            z_hx = jnp.where(bottom, 0.0, turn(hx, WIDE, 1))
            z_hy = jnp.where(bottom, 0.0, turn(hy, WIDE, 1))
            y_hx, y_hz = turn(hx, 1, 1), turn(hz, 1, 1)
            rolled = alone_rolled(main, instant, depth, False)
            back = curl_of_magnetic(hx, hy, hz, y_hx, y_hz, z_hx, z_hy)
            amount = plane_amount(table, instant, depth, depth)
            strip[0] = strip[0] + strip[6] * (back[0] + amount * strip[7])
            strip[1] = strip[1] + strip[6] * back[1]
            strip[2] = strip[2] + strip[6] * back[2]
            alone_electric(
                main,
                instant,
                depth,
                rolled,
                lambda p: cells[p],
                lambda p: plane_amount(table, instant, p, depth) * cells[depth],
            )
        for c in range(2):
            item = 2 * instant + c
            here = lane // GROUP == item
            upward = jnp.where(here, turn(strip[3 + c], GROUP * item - WIDE * (depth - 1) - TILE, 1), upward)
            downward = jnp.where(here, turn(electric[c], GROUP * item - TILE, 1), downward)
    to_a[0:wide, :] = jnp.where(even, upward, downward)
    to_b[0:wide, :] = jnp.where(even, downward, upward)
    def send(at, up, down):
        if at < to_a.shape[0]:
            to_a[at : at + TILE, :] = jnp.where(even, up, down)
        if at < to_b.shape[0]:
            to_b[at : at + TILE, :] = jnp.where(even, down, up)

    at = wide + TILE * TRACES
    for beyond in range(BEYOND):
        send(at, halo[6 * depth + depth - 1 - beyond], halo[6 * depth + beyond])
        at += TILE
    side = lanes // (BEYOND * GROUP)
    tile_lane = lane_ids((TILE, lanes))
    for begin in range(0, wide // TILE, side):
        up = jnp.zeros((TILE, lanes), F32)
        down = jnp.zeros((TILE, lanes), F32)
        for tile in range(begin, min(begin + side, wide // TILE)):
            value = strips[6, TILE * tile : TILE * (tile + 1), :]
            for beyond in range(BEYOND):
                goal = GROUP * (BEYOND * (tile - begin) + beyond)
                here = tile_lane // GROUP == goal // GROUP
                z = depth - BEYOND + beyond
                up = jnp.where(here, turn(value, goal - WIDE * z - TILE, 1), up)
                down = jnp.where(here, turn(value, goal - WIDE * beyond - TILE, 1), down)
        send(at, up, down)
        at += TILE


def received(a, b, above, here):
    even = is_even("gz")
    one, two = (a, b) if above else (b, a)
    place = lax.axis_index("gz")
    exists = place < lax.axis_size("gz") - 1 if above else place > 0
    return jnp.where(exists, jnp.where(even, one[here], two[here]), 0.0)


def coef_beyond(a, b, above, p, depth, table, shape):
    size = lax.axis_size("gz")
    first, end = pillars(depth, size)
    z = lax.axis_index("gz") * depth + p - BEYOND
    base = HALO * (depth + 2)
    quarter = COURANT * COURANT
    low, high = quarter / table[base + 1 : base + 2, :], quarter / table[base : base + 1, :]
    layer = jnp.broadcast_to(jnp.where(z < first, low, high), shape)
    one = layer if a is None else a()
    two = layer if b is None else b()
    even = is_even("gz")
    value = jnp.where(even, one, two) if above else jnp.where(even, two, one)
    return jnp.where(jnp.logical_and(z >= 0, z < depth * size), value, 0.0)


def edges_after(ex_shifted, ez, lane):
    return jnp.where(lax.rem(lane, GROUP) == HALO - 1, ex_shifted, ez)


def edges_before(hx_shifted, hz, lane):
    return jnp.where(lax.rem(lane, GROUP) == 3 * HALO, hx_shifted, hz)


def arrived_kernel(*refs):
    pass


def rolled_after(main, mixed, planes, lane):
    end = lane.shape[1] - 1
    edge = {p: turn(mixed, -(GROUP * p + HALO), 1) for p in planes}
    ex = {p: turn(main[0, p], -1, 1) for p in planes}
    ez = {p: turn(jnp.where(lane == 0, edge[p], main[2, p]), -1, 1) for p in planes}
    return {p: (jnp.where(lane == end, edge[p], ex[p]), ez[p]) for p in planes}


def rolled_before(main, mixed, planes, lane):
    end = lane.shape[1] - 1
    edge = {p: turn(mixed, -(GROUP * p + 3 * HALO), 1) for p in planes}
    hx = {p: turn(main[3, p], 1, 1) for p in planes}
    hz = {p: turn(jnp.where(lane == end, edge[p], main[5, p]), 1, 1) for p in planes}
    return {p: (jnp.where(lane == 0, edge[p], hx[p]), hz[p]) for p in planes}


def below_factors(group):
    factor = jnp.where(lax.axis_index("gz") > 0, 1.0, 0.0)
    return factor, jnp.where(group < BEYOND, factor, 1.0)


def wide_field(fields, halo, c, z):
    depth = fields.shape[1]
    own = fields[c, z] * slab_scale(c) if c >= 3 else fields[c, z]
    return jnp.concatenate([own, halo[depth * c + z]], axis=0)


def prepare_kernel(fields, halo, wide_strips, early, strips, magnetic, shifted, out):
    _, wide, lanes = wide_strips.shape
    depth = lanes // WIDE
    first, last = BEYOND, BEYOND + depth - 1
    lane = lane_ids((TILE, lanes))
    for at in range(0, wide, TILE):
        here = pl.ds(at, TILE)
        for c in range(8):
            value = wide_strips[c, here, :]
            moved = jnp.zeros((TILE, lanes), F32)
            for z in range(depth):
                goal = GROUP * (z + BEYOND)
                moved = jnp.where(lane // GROUP == z + BEYOND, turn(value, goal - WIDE * z - TILE, 1), moved)
            strips[c, here, :] = moved
    lane = lane_ids((wide, lanes))
    below_factor, strip_factor = below_factors(lane // GROUP)
    ex, ey, ez, hx, hy, hz = [strips[c] for c in range(6)]
    y_ex, y_ez = turn(ex, -1, 1), turn(ez, -1, 1)
    curl = curl_of_electric(ex, ey, ez, y_ex, y_ez, turn(ex, -GROUP, 1), turn(ey, -GROUP, 1))
    hx, hy, hz = [value - strip_factor * curl[c] for c, value in enumerate((hx, hy, hz))]
    for c, value in enumerate((hx, hy, hz)):
        magnetic[c, depth + 1] = value
    zero = jnp.zeros((wide, lanes), F32)
    main = {(c, first + z): wide_field(fields, halo, c, z) for c in range(6) for z in range(depth)}
    for c in range(6):
        main[c, first - 1] = main[c, last + 1] = zero
    moved = rolled_after(main, edges_after(y_ex, ez, lane), range(first, last + 1), lane)
    mixed = edges_before(turn(hx, 1, 1), hz, lane)
    for p in range(first - 1, last + 1):
        curl = curl_of_electric(
            main[0, p], main[1, p], main[2, p], *moved.get(p, (zero, zero)), main[0, p + 1], main[1, p + 1]
        )
        for c in range(3):
            main[3 + c, p] = main[3 + c, p] - (curl[c] if p >= first else below_factor * curl[c])
            magnetic[c, p - first + 1] = main[3 + c, p]
    moved = rolled_before(main, mixed, range(first - 1, last), lane)
    for p in range(first - 1, last):
        shifted[0, p - first + 1], shifted[1, p - first + 1] = moved[p]


def window_kernel(
    fields,
    coef,
    profile,
    halo,
    table,
    strips,
    magnetic,
    shifted,
    early_a,
    early_b,
    late_a,
    late_b,
    forward,
    material,
    fields_out,
    eps_grad,
    results,
    grad,
    sems,
    *beside,
):
    depth, rows, lanes = material.shape
    wide = rows + TILE
    shape = (wide, lanes)
    own = range(BEYOND, BEYOND + depth)
    first, last = own[0], own[-1]
    lane = lane_ids(shape)
    group = lane // GROUP

    late_strips = [received(late_a, late_b, above, slice(0, wide)) for above in (False, True)]
    places, early_end = early_rows(rows)
    traces = {}

    def merge(above, item):
        lost = item // 2 if above else item // 2 + 1
        whole = beside[TRACES * above + item]
        at, low, high = places[item]
        whole[low:high, :] = received(early_a, early_b, above, slice(at, at + high - low))
        at = wide + TILE * item
        right = received(late_a, late_b, above, slice(at, at + HALO))
        left = received(late_a, late_b, above, slice(at + HALO, at + TILE))
        whole[rows - lost : rows - lost + HALO, :] = right
        if lost < HALO:
            whole[rows + HALO + lost : wide, :] = left[0 : HALO - lost]
        if lost > 0:
            whole[0:lost, :] = left[HALO - lost : HALO]
        value = whole[...]
        if lost > 0:
            edge = turn(late_strips[above], lanes - HALO - GROUP * item, 1)
            value = jnp.where(lane >= lanes - lost, edge, value)
        lost_left = lost if above else lost - 1
        if lost_left > 0:
            edge = turn(late_strips[above], -(GROUP * item + 3 * HALO), 1)
            value = jnp.where(lane < lost_left, edge, value)
        traces[above, item] = value

    def trace(above, item):
        return traces[above, item]

    def strip_neighbours(above, item, one, two):
        goal = last if above else first - 1
        moved = turn(late_strips[above], GROUP * (goal - item), 1)
        at_goal, at_next = group == goal, group == goal + 1
        by = -GROUP if above else GROUP
        if above:
            one = turn(one, by, 1)
            two = turn(jnp.where(at_next, two + moved, two), by, 1)
            return jnp.where(at_goal, one + moved, one), two
        one = turn(jnp.where(at_goal, one + moved, one), by, 1)
        two = turn(two, by, 1)
        return one, jnp.where(at_next, two + moved, two)

    at = wide + TILE * TRACES
    lates = [late if late.shape[0] > at else None for late in (late_a, late_b)]
    joined = lambda top, tile: jnp.concatenate([top, tile], axis=0)
    zero = jnp.zeros(shape, F32)

    def late_tile(here, shift=0):
        return [None if late is None else (lambda late=late: turn(late[here], shift, 1)) for late in lates]

    wide_coef = {first + z: joined(coef[z], halo[6 * depth + z]) for z in range(depth)}
    for beyond in range(BEYOND):
        for above in (False, True):
            p = last + 1 + beyond if above else first - 1 - beyond
            from_early = slice(early_end + rows * beyond, early_end + rows * (beyond + 1))
            parts = [
                None if early.shape[0] == early_end else (lambda early=early: early[from_early])
                for early in (early_a, early_b)
            ]
            top = coef_beyond(*parts, above, p, depth, table, (rows, lanes))
            parts = late_tile(slice(at, at + TILE))
            wide_coef[p] = joined(top, coef_beyond(*parts, above, p, depth, table, (TILE, lanes)))
        at += TILE
    side = lanes // (BEYOND * GROUP)
    tile_group = lane_ids((TILE, lanes)) // GROUP
    tiles = []
    for tile in range(wide // TILE):
        here = slice(at + TILE * (tile // side), at + TILE * (tile // side) + TILE)
        start = BEYOND * GROUP * (tile % side)
        value = strips[6, TILE * tile : TILE * (tile + 1), :]
        low = coef_beyond(*late_tile(here, -start), False, tile_group, depth, table, (TILE, lanes))
        parts = late_tile(here, GROUP * (last + 1) - start)
        high = coef_beyond(*parts, True, tile_group, depth, table, (TILE, lanes))
        value = jnp.where(tile_group < first, low, value)
        tiles.append(jnp.where(tile_group > last, high, value))
    strip_coef = jnp.concatenate(tiles, axis=0)
    wide_profile = joined(profile[...], halo[7 * depth])
    strip = [strips[c] for c in range(6)]
    main = {(c, p): zero for c in range(6) for p in range(first - BEYOND, last + BEYOND + 1)}
    for c in range(3):
        for z in range(depth):
            main[c, first + z] = wide_field(fields, halo, c, z)
        for p in range(first - 1, last + 1):
            main[3 + c, p] = magnetic[c, p - first + 1]
        strip[3 + c] = magnetic[c, depth + 1]
    below_factor, strip_factor = below_factors(group)

    copies = []

    def hand_out(source, target):
        copy = pltpu.make_async_copy(source, target, sems.at[len(copies)])
        copy.start()
        copies.append(copy)

    def magnetic_planes(instant):
        above = min(instant, HALO - 1 - instant, BEYOND - 1)
        return list(range(first - min(instant + 1, HALO - instant, BEYOND), last + above + 1))

    def electric_planes(instant):
        reach = min(instant + 1, HALO - 1 - instant, BEYOND)
        return list(range(first - reach, last + reach + 1))

    def in_groups(planes):
        size = -(-len(planes) // GROUPS)
        return [planes[at : at + size] for at in range(0, len(planes), size)]

    def strip_magnetic(instant):
        ex, ey, ez = strip[0:3]
        curl = curl_of_electric(ex, ey, ez, *strip_shifts)
        for c in range(3):
            strip[3 + c] = strip[3 + c] - strip_factor * curl[c]
        return strip_shifted_magnetic(instant)

    def strip_shifted_magnetic(instant):
        hx, hy, hz = strip[3:6]
        y_hx, y_hz = turn(hx, 1, 1), turn(hz, 1, 1)
        z_hx, z_hy = strip_neighbours(False, 2 * instant, hx, hy)
        return (y_hx, y_hz, z_hx, z_hy), edges_before(y_hx, hz, lane)

    def strip_shifted_electric(instant):
        ex, ey, ez = strip[0:3]
        y_ex, y_ez = turn(ex, -1, 1), turn(ez, -1, 1)
        z_ex, z_ey = strip_neighbours(True, 2 * instant, ex, ey)
        return (y_ex, y_ez, z_ex, z_ey), edges_after(y_ex, ez, lane)

    def strip_electric(instant):
        back = curl_of_magnetic(*strip[3:6], *strip_shifts)
        amount = plane_amount(table, instant, depth + 1, depth)
        strip[0] = strip[0] + strip_coef * (back[0] + amount * strips[7])
        strip[1] = strip[1] + strip_coef * back[1]
        strip[2] = strip[2] + strip_coef * back[2]
        return strip_shifted_electric(instant + 1)

    total = [None] * depth
    merge(True, 0)
    merge(True, 1)
    at_last = group == last
    strip[3] = jnp.where(at_last, strip[3] + turn(late_strips[True], GROUP * (last - 1), 1), strip[3])
    strip[4] = jnp.where(at_last, strip[4] - turn(late_strips[True], GROUP * last, 1), strip[4])
    main[3, last] = main[3, last] + trace(True, 1)
    main[4, last] = main[4, last] - trace(True, 0)
    strip_shifts, mixed = strip_shifted_magnetic(0)
    moved = {p: (shifted[0, p - first + 1], shifted[1, p - first + 1]) for p in range(first - 1, last)}
    moved[last + 1] = (zero, zero)
    for instant in range(HALO):
        item = 2 * instant
        final = instant == HALO - 1

        mixed_now = mixed
        if not final:
            strip_shifts, mixed = strip_electric(instant)
        merge(False, item)
        merge(False, item + 1)
        if instant == 0:
            moved.update(rolled_before(main, mixed_now, [last], lane))
        else:
            following = electric_planes(instant)
            later = {p: (zero, zero) for p in following}
            for planes in in_groups(magnetic_planes(instant)):
                for p in planes:
                    z_ex, z_ey = main[0, p + 1], main[1, p + 1]
                    if p == last:
                        z_ex, z_ey = z_ex + trace(True, item), z_ey + trace(True, item + 1)
                    curl = curl_of_electric(
                        main[0, p], main[1, p], main[2, p], *moved.get(p, (zero, zero)), z_ex, z_ey
                    )
                    for c in range(3):
                        main[3 + c, p] = main[3 + c, p] - (curl[c] if p >= first else below_factor * curl[c])
                        if final and first <= p <= last:
                            results[3 + c, p - first] = main[3 + c, p][0:rows] * COURANT
                    if final and first <= p <= last:
                        z = p - first
                        hand_out(results.at[pl.ds(3, 3), z], fields_out.at[pl.ds(3, 3), z])
                later.update(rolled_before(main, mixed_now, [p for p in planes if p in following], lane))
            moved = later

        mixed_now = mixed
        if not final:
            strip_shifts, mixed = strip_magnetic(instant + 1)
            merge(True, item + 2)
            merge(True, item + 3)
        following = [] if final else magnetic_planes(instant + 1)
        later = {}
        for planes in in_groups(electric_planes(instant)):
            for p in planes:
                z_hx, z_hy = main.get((3, p - 1), zero), main.get((4, p - 1), zero)
                if p == first:
                    z_hx, z_hy = z_hx + trace(False, item), z_hy + trace(False, item + 1)
                back = curl_of_magnetic(main[3, p], main[4, p], main[5, p], *moved[p], z_hx, z_hy)
                here = wide_coef[p]
                inside = first <= p <= last
                z = p - first
                if inside:
                    push = plane_amount(table, instant, z, depth) * wide_profile
                    back = (back[0] + push, back[1], back[2])
                for c in range(3):
                    main[c, p] = main[c, p] + here * back[c]
                    if inside:
                        term = forward[instant, c, z].astype(F32) * main[c, p][0:rows]
                        total[z] = term if total[z] is None else total[z] + term
                if inside and final:
                    for c in range(3):
                        results[c, z] = main[c, p][0:rows]
                    grad[z] = jnp.where(material[z] >= 2, -total[z], 0.0)
                    hand_out(results.at[pl.ds(0, 3), z], fields_out.at[pl.ds(0, 3), z])
                    hand_out(grad.at[z], eps_grad.at[z])
            later.update(rolled_after(main, mixed_now, [p for p in planes if p in following], lane))
        moved = later
    for copy in copies:
        copy.wait()


VMEM = pl.BlockSpec(memory_space=pltpu.VMEM)
FAR = pl.BlockSpec(memory_space=pltpu.HBM)


def near(array):
    return pltpu.with_memory_space_constraint(array, pltpu.VMEM)


def far_off(array):
    return pltpu.with_memory_space_constraint(array, pltpu.HBM), FAR


def call(kernel, operands, outs, scratch=(), far=0, aliases=None, name=None, cost=None):
    specs, arrays = [], []
    for operand in operands:
        if isinstance(operand, tuple):
            specs.append(operand[1])
            arrays.append(operand[0])
        else:
            specs.append(VMEM)
            arrays.append(near(operand))
    return pl.pallas_call(
        kernel,
        out_shape=[jax.ShapeDtypeStruct(s, F32) for s in outs[:far]] + [
            pltpu.VMEM(getattr(s, "shape", s), getattr(s, "dtype", F32)) for s in outs[far:]
        ],
        in_specs=specs,
        out_specs=[FAR] * far + [VMEM] * (len(outs) - far),
        scratch_shapes=[s if not isinstance(s, tuple) else pltpu.VMEM(s, F32) for s in scratch],
        input_output_aliases=aliases or {},
        compiler_params=pltpu.CompilerParams(vmem_limit_bytes=32 * 1024 * 1024),
        cost_estimate=cost,
        name=name,
    )(*arrays)


def on_device(
    fields_in, material, material_eps, source_plane, source_wave, source_profile, forward_fields
):
    depth, rows, lanes = material.shape
    assert source_wave.shape[0] == HALO and depth * WIDE == lanes and BEYOND <= depth
    assert (depth + 2 * BEYOND) * GROUP == lanes and TRACES * GROUP == lanes
    wide = rows + TILE
    slabs = 7 * depth + 1
    tiles = (slabs + 1) // 2

    inputs = (fields_in, material, source_profile, material_eps, source_wave)
    to_a, to_b, scalars, material, source_profile = call(
        x_pack_kernel,
        [far_off(array) for array in inputs],
        [(tiles, TILE, lanes)] * 2
        + [(HALO + material_eps.shape[0], lanes), material, source_profile.shape],
        [
            (2, 6, depth, TILE, lanes),
            pltpu.SMEM(material_eps.shape, F32),
            pltpu.SMEM(source_wave.shape, F32),
            pltpu.SemaphoreType.DMA((6,)),
        ],
        name="x_pack",
    )
    swap_a, swap_b = swaps(lax.axis_size("gx"), True)
    from_b = lax.ppermute(to_b, "gx", swap_b)
    from_a = lax.ppermute(to_a, "gx", swap_a)

    pairs_a, z_a, pairs_b, z_b = z_swaps(lax.axis_size("gz"), lax.axis_size("gx"))
    with_coef = [sends_coef(depth, lax.axis_size("gz"), pairs) for pairs in (pairs_a, pairs_b)]
    early_counts = [early_rows(rows)[1] + rows * BEYOND * sent for sent in with_coef]
    plane = jnp.broadcast_to(source_plane[None], (1, lanes))
    coef, early_a, early_b, partly, table = call(
        interior_kernel,
        [fields_in, material, source_profile, scalars, plane],
        [(depth, rows, lanes)]
        + [(count, lanes) for count in early_counts]
        + [(2, wide, lanes), (HALO * (depth + 2) + material_eps.shape[0], lanes)],
        name="interior",
    )
    halo, y_out = call(
        x_unpack_kernel,
        [from_b, from_a, partly],
        [(slabs, TILE, lanes), (2, wide, lanes)],
        aliases={2: 1},
        name="x_unpack",
    )
    swap_a, swap_b = swaps(lax.axis_size("gy"), True)
    if lax.axis_size("gy") == 2:
        both = lax.ppermute(y_out, "gy", swap_a)
        from_one, from_two = both[0], both[1]
    else:
        from_one = lax.ppermute(y_out[0], "gy", swap_a)
        from_two = lax.ppermute(y_out[1], "gy", swap_b)

    early_a = lax.ppermute(early_a, ("gz", "gx"), z_a)
    early_b = lax.ppermute(early_b, ("gz", "gx"), z_b)
    (own,) = call(
        own_strips_kernel,
        [fields_in, coef, source_profile, halo],
        [(8, wide, lanes)],
        name="own_strips",
    )
    side = lanes // (BEYOND * GROUP)
    coef_rows = TILE * BEYOND + TILE * (-(-wide // TILE // side))
    late_rows = [wide + TILE * TRACES + coef_rows * sent for sent in with_coef]
    strips, late_a, late_b = call(
        frame_kernel,
        [fields_in, coef, source_profile, table, halo, own, from_one, from_two],
        [(8, wide, lanes)] + [(count, lanes) for count in late_rows],
        name="frame",
    )
    late_a = lax.ppermute(late_a, ("gz", "gx"), z_a)
    late_b = lax.ppermute(late_b, ("gz", "gx"), z_b)

    (early_b,) = call(
        arrived_kernel,
        [early_b],
        [early_b.shape],
        aliases={0: 0},
        name="arrived",
        cost=pl.CostEstimate(flops=10**9, bytes_accessed=0, transcendentals=0),
    )
    strips, magnetic, shifted, early_b = call(
        prepare_kernel,
        [fields_in, halo, strips, early_b],
        [(8, wide, lanes), (3, depth + 2, wide, lanes), (2, depth, wide, lanes), early_b.shape],
        aliases={3: 3},
        name="prepare",
    )
    fields_out, eps_grad = call(
        window_kernel,
        [fields_in, coef, source_profile, halo, table, strips, magnetic, shifted]
        + [early_a, early_b, late_a, late_b]
        + [forward_fields, material],
        [(6, depth, rows, lanes), (depth, rows, lanes)],
        [
            (6, depth, rows, lanes),
            (depth, rows, lanes),
            pltpu.SemaphoreType.DMA((3 * depth,)),
        ]
        + [(wide, lanes)] * (2 * TRACES),
        far=2,
        name="window",
    )
    return (fields_out, eps_grad)


def solution(mesh):
    placed = (
        P(None, "gz", "gx", "gy"),
        P("gz", "gx", "gy"),
        P(),
        P(),
        P(),
        P("gx", "gy"),
        P(None, None, "gz", "gx", "gy"),
    )
    return jax.shard_map(
        on_device,
        mesh=mesh,
        in_specs=placed,
        out_specs=(P(None, "gz", "gx", "gy"), P("gz", "gx", "gy")),
        check_vma=False,
    )
```
